256 devices in a mesh: section: 2 (over core), wide: 16 (over y, z_lo), narrow: 8 (over z_hi, x).
Axes of the slice: x: 4, y: 4, z: 8 (z_hi: 2, z_lo: 4; z = z_hi * 4 + z_lo), core: 2. Of those that a mesh axis runs over, the one named last changes fastest.
Arguments:
- section_input: bfloat16 [2, 16, 14, 14, 2560], P('section', 'narrow', None, None, 'wide'), may hold values from -6 to 6
- kernels: bfloat16 [2, 3, 3, 2560, 2560], P('section', None, None, 'wide', 'narrow'), may hold values from -0.0390625 to 0.0390625
Outputs:
- section_out: bfloat16 [2, 16, 14, 14, 2560], P('section', 'narrow', None, None, 'wide')
- kernel_grads: float32 [2, 3, 3, 2560, 2560], P('section', None, None, 'wide', 'narrow')
The draws below stay inside these ranges and needn't reach their ends.
All inputs are finite; a program needn't handle non-finite values.
Results may differ from the reference program's by a relative error of at most 0.0054.
Values may be sent and summed in bfloat16 or wider, within the bound.
A program may use at most 64 MiB of HBM per device.

```python
import math
import jax
import jax.numpy as jnp

CH = 2560
SIDE = 14
IMAGES = 16


def block_scale(rng, shape, shards, smallest, high):
    gain = 1.0
    for position, shards_of in shards:
        heights = jax.random.uniform(jax.random.fold_in(jax.random.fold_in(rng, 6), position), (shards_of,), jnp.float32, smallest / len(shards), high / len(shards))
        gain = gain * jnp.repeat(jnp.exp(heights), shape[position] // shards_of).reshape((-1,) + (1,) * (len(shape) - 1 - position))
    return gain


def noise(rng, shape, spread, bound, pieces=(), held_as=jnp.bfloat16):
    level = block_scale(rng, shape, pieces, -0.22, 0.18) if pieces else 1.0
    drawn = jax.random.normal(rng, shape, jnp.float32) * spread * level
    return jnp.minimum(jnp.maximum(drawn, -bound), bound).astype(held_as)


def setup_inputs(seed: int = 0) -> dict:
    key_list = jax.random.split(jax.random.key(seed), 3)
    section_input = noise(key_list[0], (2, IMAGES, SIDE, SIDE, CH), 1.0, 6.0, ((0, 2), (1, 8), (4, 16)))
    kernels = noise(key_list[1], (2, 3, 3, CH, CH), (9 * CH) ** -0.5, 0.0390625, ((0, 2), (3, 16), (4, 8)))
    return {"section_input": section_input, "kernels": kernels}


def shifted(values, tap_row, tap_col):
    extent = values.shape[1]
    padded = jnp.pad(values, ((0, 0), (1, 1), (1, 1), (0, 0)))
    return padded[:, tap_row:tap_row + extent, tap_col:tap_col + extent, :]

def convolve(values, kernel):
    amount, extent = (values.shape[0], values.shape[1])
    flat_rows = amount * extent * extent
    total = jnp.zeros((flat_rows, kernel.shape[3]), jnp.float32)
    for tap_row in range(3):
        for tap_col in range(3):
            window = shifted(values, tap_row, tap_col).reshape(flat_rows, values.shape[3])
            total = total + jnp.dot(window, kernel[tap_row, tap_col], preferred_element_type=jnp.float32)
    return total.reshape(amount, extent, extent, kernel.shape[3])

def correlate(values, partner):
    amount, extent = (values.shape[0], values.shape[1])
    flat_rows = amount * extent * extent
    flat_partner = partner.reshape(flat_rows, partner.shape[3])
    tap_list = []
    for tap_row in range(3):
        for tap_col in range(3):
            window = shifted(values, tap_row, tap_col).reshape(flat_rows, values.shape[3])
            tap_list.append(jnp.dot(window.T, flat_partner, preferred_element_type=jnp.float32))
    return jnp.stack(tap_list).reshape(3, 3, values.shape[3], partner.shape[3])

def flipped(kernel):
    return kernel[::-1, ::-1]

def smooth(values):
    return values * jax.nn.sigmoid(values)

def smooth_slope(values):
    logistic = jax.nn.sigmoid(values)
    return logistic * (1.0 + values * (1.0 - logistic))

def reference(section_input, kernels):
    images = section_input[0]
    out_grad = section_input[1]
    kernel_a = kernels[0]
    kernel_b = jnp.swapaxes(kernels[1], 2, 3)
    pre_act = convolve(images, kernel_a)
    boundary_act = smooth(pre_act).astype(jnp.bfloat16)
    boundary_grad = convolve(out_grad, flipped(kernels[1])).astype(jnp.bfloat16)
    act_grad = (boundary_grad.astype(jnp.float32) * smooth_slope(pre_act)).astype(jnp.bfloat16)
    section_output = convolve(boundary_act, kernel_b).astype(jnp.bfloat16)
    input_grad = convolve(act_grad, flipped(jnp.swapaxes(kernel_a, 2, 3))).astype(jnp.bfloat16)
    grad_scale = 1.0 / math.sqrt(IMAGES * SIDE * SIDE)
    grad_a = correlate(images, act_grad) * grad_scale
    grad_b = jnp.swapaxes(correlate(boundary_act, out_grad), 2, 3) * grad_scale
    return (jnp.stack([input_grad, section_output]), jnp.stack([grad_a, grad_b]))
```

```python
import functools
import math

import jax
import jax.numpy as jnp
from jax import lax
from jax.experimental import pallas as pl
from jax.experimental.pallas import tpu as pltpu
from jax.sharding import PartitionSpec as P

MESH = pl.DeviceIdType.MESH

SIDE = 14
LANES = 512
CHUNKS = 8
TAPS = 9
BF16 = jnp.bfloat16
F32 = jnp.float32

SLOT = {(0, 0): 0, (0, 1): 1, (1, 0): 2, (1, 1): 3, (1, 3): 4, (1, 2): 5, (0, 3): 6, (0, 2): 7}


def chunk_dz(k):
    return ((k + 2) // 4) % 2


def chunk_dx(k):
    low = k % 2
    return low + (k // 4) * (3 - 2 * low)


def silu(values):
    return values * jax.nn.sigmoid(values)


def silu_slope(values):
    logistic = jax.nn.sigmoid(values)
    return logistic * (1.0 + values * (1.0 - logistic))


def tap_offset(tap):
    return (tap // 3 - 1) * 16 + (tap % 3 - 1)


def kernel(
    scale,
    x_ref,
    k_ref,
    out_ref,
    grad_ref,
    wide_x,
    taps,
    flipped,
    part,
    part_f,
    got_y,
    quarter,
    quarter_f,
    got_z,
    pre,
    ex_out,
    ex_in,
    act,
    act_all,
    products,
    share,
    got_x,
    own_sum,
    pair_out,
    pair_in,
    s_img,
    r_img,
    s_y,
    r_y,
    s_z,
    r_z,
    s_ex,
    r_ex,
    s_az,
    r_az,
    s_ay,
    r_ay,
    s_share,
    r_share,
    s_pair,
    r_pair,
):
    section = lax.axis_index("section")
    wide = lax.axis_index("wide")
    narrow = lax.axis_index("narrow")
    y, zl = wide // 4, wide % 4
    zh, x = narrow // 4, narrow % 4

    def at_y(j):
        return (section, ((y + j) % 4) * 4 + zl, narrow)

    def at_z(j):
        return (section, y * 4 + (zl + j) % 4, narrow)

    def at_x(j):
        return (section, wide, zh * 4 + (x + j) % 4)

    pair = (section, wide, (1 - zh) * 4 + x)
    other = (1 - section, wide, narrow)

    def copy(src, dst, send, recv, device):
        return pltpu.make_async_remote_copy(
            src_ref=src, dst_ref=dst, send_sem=send, recv_sem=recv, device_id=device, device_id_type=MESH
        )

    barrier = pltpu.get_barrier_semaphore()
    peers = [at_y(j) for j in (1, 2, 3)] + [at_z(j) for j in (1, 2, 3)]
    peers += [at_x(j) for j in (1, 2, 3)] + [pair, other]
    for peer in peers:
        pl.semaphore_signal(barrier, inc=1, device_id=peer, device_id_type=MESH)

    blank = jnp.zeros((SIDE, 2, x_ref.shape[2]), BF16)
    rows = []
    for image in range(2):
        tile = x_ref[image * SIDE : (image + 1) * SIDE]
        tile = jnp.concatenate([tile, blank], axis=1)
        rows.append(tile.reshape(SIDE * 16, x_ref.shape[2]))
        rows.append(jnp.zeros((32, x_ref.shape[2]), BF16))
    wide_x[0] = jnp.concatenate(rows, axis=0).T

    pl.semaphore_wait(barrier, len(peers))

    def image_copy(slot, dz, j):
        there = SLOT[(dz, (4 - j) % 4)]
        return copy(wide_x.at[slot], wide_x.at[there], s_img.at[there], r_img.at[there], at_x(j))

    to_pair = copy(wide_x.at[0], wide_x.at[2], s_img.at[2], r_img.at[2], pair)
    to_pair.start()
    image_copy(0, 0, 3).start()

    flipped[...] = k_ref[...].T
    grad_ref[...] = jnp.zeros_like(grad_ref)

    sign = 1 - 2 * section
    lane = lax.broadcasted_iota(jnp.int32, (1, 128), 1)
    row = (zl % 2) * 8 + lane // 16
    inside = ((lane % 16 < SIDE) & (row < SIDE)).astype(F32)

    def shift_of(tap, direction):
        return (LANES - direction * tap_offset(tap)) % LANES

    def y_copy(k, j):
        return copy(
            part.at[k, (y + j) % 4], got_y.at[k, j - 1], s_y.at[k, j - 1], r_y.at[k, j - 1], at_y(j)
        )

    def z_copy(k, j):
        return copy(
            quarter.at[k, (zl + j) % 4], got_z.at[k, j - 1], s_z.at[k, j - 1], r_z.at[k, j - 1], at_z(j)
        )

    def ex_copy(k):
        return copy(ex_out.at[k], ex_in.at[k], s_ex.at[k], r_ex.at[k], other)

    def az_copy(k, j):
        here = act.at[k, y, zl]
        return copy(here, here, s_az.at[k, j - 1], r_az.at[k, j - 1], at_z(j))

    def ay_copy(k, j):
        here = act.at[k, y]
        return copy(here, here, s_ay.at[k, j - 1], r_ay.at[k, j - 1], at_y(j))

    def share_copy(k):
        dz, dx = chunk_dz(k), chunk_dx(k)
        slot = 3 - dx
        return copy(share.at[k], got_x.at[dz, slot], s_share.at[k], r_share.at[dz, slot], at_x(dx))

    def arrived(buffer, send, recv, device):
        copy(buffer, buffer, send, recv, device).wait_recv()

    def first_conv(k):
        @pl.when((k > 0) & (k != 2))
        def _():
            arrived(wide_x.at[k], s_img.at[k], r_img.at[k], pair)

        image = wide_x[k]
        for tap in range(TAPS):
            moved = image if tap == 4 else pltpu.roll(image, shift_of(tap, sign), 1)
            taps[k, pl.ds(160 * tap, 160), :] = moved
        total = jnp.dot(flipped[...], taps[k], preferred_element_type=F32)
        for block in range(4):
            piece = total[80 * block : 80 * block + 80]
            part_f[k % 2, block] = piece
            part[k, block] = piece.astype(BF16)
        for j in (1, 3, 2):
            y_copy(k, j).start()

    def sum_y(k):
        for j in (1, 2, 3):
            arrived(got_y.at[k, j - 1], s_y.at[k, j - 1], r_y.at[k, j - 1], at_y(j))
        total = part_f[k % 2, y]
        for j in range(3):
            total = total + got_y[k, j].astype(F32)
        for block in range(4):
            piece = total[:, 128 * block : 128 * block + 128]
            quarter_f[k % 2, block] = piece
            quarter[k, block] = piece.astype(BF16)
        for j in (1, 2, 3):
            z_copy(k, j).start()

    def sum_z(k):
        for j in (1, 2, 3):
            arrived(got_z.at[k, j - 1], s_z.at[k, j - 1], r_z.at[k, j - 1], at_z(j))
        total = quarter_f[k % 2, zl]
        for j in range(3):
            total = total + got_z[k, j].astype(F32)
        pre[k] = total
        sent = jnp.where(section == 0, silu(total), total) * inside
        ex_out[k] = sent.astype(BF16)
        ex_copy(k).start()

    def meet(k):
        arrived(ex_in.at[k], s_ex.at[k], r_ex.at[k], other)
        incoming = ex_in[k].astype(F32)
        received = jnp.where(section == 0, incoming * silu_slope(pre[k]), incoming)
        act[k, y, zl] = received.astype(BF16)
        for j in (1, 2, 3):
            az_copy(k, j).start()

    def spread_y(k):
        for j in (1, 2, 3):
            arrived(act.at[k, y, (zl + j) % 4], s_az.at[k, j - 1], r_az.at[k, 3 - j], at_z(j))
        for j in (1, 3, 2):
            ay_copy(k, j).start()

    def second_conv(k):
        for j in (1, 2, 3):
            arrived(act.at[k, (y + j) % 4], s_ay.at[k, j - 1], r_ay.at[k, 3 - j], at_y(j))
        for a in range(4):
            for b in range(4):
                act_all[pl.ds(80 * a, 80), pl.ds(128 * b, 128)] = act[k, a, b]
        products[...] = jnp.dot(k_ref[...], act_all[...], preferred_element_type=F32)
        total = products[pl.ds(160 * 4, 160), :]
        for tap in range(TAPS):
            if tap != 4:
                moved = pltpu.roll(products[pl.ds(160 * tap, 160), :], shift_of(tap, -sign), 1)
                total = total + moved
        dx = chunk_dx(k)

        @pl.when(dx == 0)
        def _():
            own_sum[chunk_dz(k)] = total

        @pl.when(dx != 0)
        def _():
            share[k] = total.astype(BF16)
            share_copy(k).start()

        grad_ref[...] += lax.dot_general(
            taps[k], act_all[...], (((1,), (1,)), ((), ())), preferred_element_type=F32
        )

    def sum_x(dz):
        total = own_sum[dz]
        for j in range(3):
            arrived(got_x.at[dz, j], s_share.at[1], r_share.at[dz, j], at_x(1))
            total = total + got_x[dz, j].astype(F32)
        return total

    def step(t, carry):
        @pl.when(t < CHUNKS)
        def _():
            first_conv(t)

        @pl.when(t == 0)
        def _():
            image_copy(0, 0, 1).start()
            image_copy(0, 0, 2).start()

        @pl.when(t == 1)
        def _():
            arrived(wide_x.at[2], s_img.at[2], r_img.at[2], pair)
            for j in (3, 1, 2):
                image_copy(2, 1, j).start()

        for lag, stage in ((4, spread_y), (3, meet), (2, sum_z), (1, sum_y), (5, second_conv)):

            @pl.when((t >= lag) & (t < CHUNKS + lag))
            def _():
                stage(t - lag)

        return carry

    lax.fori_loop(0, CHUNKS + 5, step, 0)

    pair_out[...] = sum_x(1).astype(BF16)
    across = copy(pair_out, pair_in, s_pair, r_pair, pair)
    across.start()
    grad_ref[...] *= scale
    total = sum_x(0)
    across.wait_recv()
    total = (total + pair_in[...].astype(F32)).astype(BF16)
    turned = total.T.reshape(LANES // 16, 16, out_ref.shape[2])
    for image in range(2):
        out_ref[image * SIDE : (image + 1) * SIDE] = turned[16 * image : 16 * image + SIDE, :SIDE]

    across.wait_send()
    to_pair.wait_send()
    for j in (1, 2, 3):
        image_copy(0, 0, j).wait_send()
        image_copy(2, 1, j).wait_send()

    def finish(k, carry):
        for j in (1, 2, 3):
            y_copy(k, j).wait_send()
            z_copy(k, j).wait_send()
            az_copy(k, j).wait_send()
            ay_copy(k, j).wait_send()
        ex_copy(k).wait_send()

        @pl.when(chunk_dx(k) != 0)
        def _():
            share_copy(k).wait_send()

        return carry

    lax.fori_loop(0, CHUNKS, finish, 0)


def body(section_input, kernels):
    images, channels = section_input.shape[1], section_input.shape[4]
    inner = kernels.shape[4]
    scale = 1.0 / math.sqrt(CHUNKS * images * SIDE * SIDE)
    sem = pltpu.SemaphoreType.DMA
    out, grads = pl.pallas_call(
        functools.partial(kernel, scale),
        out_shape=(
            jax.ShapeDtypeStruct((images * SIDE, SIDE, channels), BF16),
            jax.ShapeDtypeStruct((TAPS * channels, inner), F32),
        ),
        in_specs=[pl.BlockSpec(memory_space=pltpu.VMEM)] * 2,
        out_specs=[pl.BlockSpec(memory_space=pltpu.VMEM)] * 2,
        scratch_shapes=[
            pltpu.VMEM((CHUNKS, channels, LANES), BF16),
            pltpu.VMEM((CHUNKS, TAPS * channels, LANES), BF16),
            pltpu.VMEM((inner, TAPS * channels), BF16),
            pltpu.VMEM((CHUNKS, 4, 80, LANES), BF16),
            pltpu.VMEM((2, 4, 80, LANES), F32),
            pltpu.VMEM((CHUNKS, 3, 80, LANES), BF16),
            pltpu.VMEM((CHUNKS, 4, 80, 128), BF16),
            pltpu.VMEM((2, 4, 80, 128), F32),
            pltpu.VMEM((CHUNKS, 3, 80, 128), BF16),
            pltpu.VMEM((CHUNKS, 80, 128), F32),
            pltpu.VMEM((CHUNKS, 80, 128), BF16),
            pltpu.VMEM((CHUNKS, 80, 128), BF16),
            pltpu.VMEM((CHUNKS, 4, 4, 80, 128), BF16),
            pltpu.VMEM((inner, LANES), BF16),
            pltpu.VMEM((TAPS * channels, LANES), F32),
            pltpu.VMEM((CHUNKS, channels, LANES), BF16),
            pltpu.VMEM((2, 3, channels, LANES), BF16),
            pltpu.VMEM((2, channels, LANES), F32),
            pltpu.VMEM((channels, LANES), BF16),
            pltpu.VMEM((channels, LANES), BF16),
            sem((CHUNKS,)),
            sem((CHUNKS,)),
            sem((CHUNKS, 3)),
            sem((CHUNKS, 3)),
            sem((CHUNKS, 3)),
            sem((CHUNKS, 3)),
            sem((CHUNKS,)),
            sem((CHUNKS,)),
            sem((CHUNKS, 3)),
            sem((CHUNKS, 3)),
            sem((CHUNKS, 3)),
            sem((CHUNKS, 3)),
            sem((CHUNKS,)),
            sem((2, 3)),
            sem,
            sem,
        ],
        compiler_params=pltpu.CompilerParams(
            collective_id=0, has_side_effects=True, vmem_limit_bytes=60 * 2**20
        ),
        name="relay",
    )(
        section_input.reshape(images * SIDE, SIDE, channels),
        kernels.reshape(TAPS * channels, inner),
    )
    return (
        out.reshape(section_input.shape),
        grads.reshape(kernels.shape),
    )


def solution(mesh):
    return jax.shard_map(
        body,
        mesh=mesh,
        in_specs=(
            P("section", "narrow", None, None, "wide"),
            P("section", None, None, "wide", "narrow"),
        ),
        out_specs=(
            P("section", "narrow", None, None, "wide"),
            P("section", None, None, "wide", "narrow"),
        ),
        check_vma=False,
    )
```

```python
import math

import jax
import jax.numpy as jnp
from jax import lax
from jax.experimental import pallas as pl
from jax.experimental.pallas import tpu as pltpu
from jax.sharding import PartitionSpec as P

MESH = pl.DeviceIdType.MESH
BF16 = jnp.bfloat16
F32 = jnp.float32

SIDE = 14
CHUNKS = 8
PIXELS = 2 * SIDE * SIDE
LANES = 512
SPILL = PIXELS - 384
TAPS = 9
ROWS_A = 160
ROWS_B = 320
BLOCK_A = 3 * ROWS_A + 16
BLOCK_B = 3 * (ROWS_B // 4) + 16
HALF = BLOCK_B // 2
QUARTER = BLOCK_B // 4

SLOT = {(0, 0): 0, (0, 1): 1, (0, 2): 2, (1, 0): 3, (1, 1): 4, (1, 2): 5, (1, 3): 6, (0, 3): 7}
FROM_PAIR = SLOT[(1, 0)]

PLAN = (
    (0, 1, "next_conv"),
    (1, 0, "join"),
    (5, 0, "spread_y"),
    (3, 0, "sum_z"),
    (6, 0, "forward_y"),
    (2, 0, "sum_y"),
    (7, 1, "second_conv"),
    (3, 0, "meet"),
    (9, 1, "kernel_grad"),
)
LAST = 7
LATE_GRADS = (6, 7, 0)


def chunk_dz(k):
    return ((k + 1) // 4) % 2


def chunk_dx(k):
    late = k // 6
    return (1 - late) * (k % 3) + 3 * late


def silu(values):
    return values * jax.nn.sigmoid(values)


def silu_slope(values):
    logistic = jax.nn.sigmoid(values)
    return logistic * (1.0 + values * (1.0 - logistic))


def pack(values):
    rows = values.shape[0]
    spilled = values[:16, 384:]
    for group in range(1, rows // 16):
        spilled = spilled + pltpu.roll(values[16 * group : 16 * group + 16, 384:], SPILL * group, 1)
    return jnp.concatenate([values[:, 0:128], values[:, 128:256], values[:, 256:384], spilled], axis=0)


def unpack(block, rows, keep):
    spilled = block[3 * rows :]
    last = [spilled * keep]
    for group in range(1, rows // 16):
        last.append(pltpu.roll(spilled, 128 - SPILL * group, 1) * keep)
    parts = [block[0:rows], block[rows : 2 * rows], block[2 * rows : 3 * rows], jnp.concatenate(last, axis=0)]
    return jnp.concatenate(parts, axis=1)


def kernel(
    x_ref,
    k_hbm,
    out_ref,
    grad_ref,
    k_ref,
    masks,
    masks_f,
    images,
    taps,
    flipped,
    part,
    part_f,
    relayed,
    joined,
    got_y,
    quarter,
    quarter_f,
    got_z,
    pre,
    ex_out,
    ex_in,
    act,
    act_all,
    products,
    share,
    got_x,
    own_sum,
    pair_out,
    pair_in,
    s_load,
    s_img,
    s_relay,
    s_near,
    s_join,
    s_z,
    s_ex,
    s_az,
    s_ay,
    s_af,
    s_share,
    s_pair,
    r_img,
    r_relay,
    r_y,
    r_z,
    r_ex,
    r_az,
    r_ay,
    r_af,
    r_share,
    r_pair,
):
    section = lax.axis_index("section")
    wide = lax.axis_index("wide")
    narrow = lax.axis_index("narrow")
    y, zl = wide // 4, wide % 4
    zh, x = narrow // 4, narrow % 4

    def at_y(j):
        return (section, ((y + j) % 4) * 4 + zl, narrow)

    def at_z(j):
        return (section, y * 4 + (zl + j) % 4, narrow)

    def at_x(j):
        return (section, wide, zh * 4 + (x + j) % 4)

    pair = (section, wide, (1 - zh) * 4 + x)
    other = (1 - section, wide, narrow)

    def copy(src, dst, send, recv, device):
        return pltpu.make_async_remote_copy(
            src_ref=src, dst_ref=dst, send_sem=send, recv_sem=recv, device_id=device, device_id_type=MESH
        )

    barrier = pltpu.get_barrier_semaphore()
    peers = [at_y(j) for j in (1, 3)] + [at_z(j) for j in (1, 2, 3)]
    peers += [at_x(j) for j in (1, 2, 3)] + [pair, other]
    for peer in peers:
        pl.semaphore_signal(barrier, inc=1, device_id=peer, device_id_type=MESH)

    load = pltpu.make_async_copy(k_hbm, k_ref, s_load)
    load.start()

    sign = 1 - 2 * section
    lane = lax.broadcasted_iota(jnp.int32, (1, LANES), 1)
    pixel = lane // 2
    row = pixel // SIDE
    column = pixel - SIDE * row
    for tap in range(TAPS):
        there_row = row + sign * (tap // 3 - 1)
        there_column = column + sign * (tap % 3 - 1)
        inside = (there_row >= 0) & (there_row < SIDE) & (there_column >= 0) & (there_column < SIDE)
        inside = (inside & (lane < PIXELS)).astype(F32)
        masks_f[tap] = inside
        masks[tap] = inside.astype(BF16)
    keep = (lane[:, :128] < SPILL).astype(BF16)

    def shift_of(tap, direction):
        offset = 2 * ((tap // 3 - 1) * SIDE + tap % 3 - 1)
        return (LANES - direction * offset) % LANES

    blank = jnp.zeros((LANES - PIXELS, ROWS_A), F32)
    own_f = jnp.concatenate([x_ref[...].astype(F32), blank], axis=0).T
    own = own_f.astype(BF16)
    images[0] = pack(own_f).astype(BF16)
    grad_ref[...] = jnp.zeros_like(grad_ref)

    def image_copy(slot, dz, j):
        there = SLOT[(dz, (4 - j) % 4)]
        return copy(images.at[slot], images.at[there], s_img, r_img.at[there], at_x(j))

    to_pair = copy(images.at[0], images.at[FROM_PAIR], s_img, r_img.at[FROM_PAIR], pair)

    def relay_copy(k, half):
        return copy(
            part.at[k, (y + 2) % 4, half], relayed.at[k, half], s_relay, r_relay.at[k], at_y(1 + 2 * half)
        )

    def near_copy(k, half):
        j = 3 - 2 * half
        return copy(part.at[k, (y + j) % 4, half], got_y.at[k, 0, half], s_near, r_y.at[k], at_y(j))

    def join_copy(k, half):
        return copy(joined.at[k, half], got_y.at[k, 1, half], s_join, r_y.at[k], at_y(1 + 2 * half))

    def z_copy(k, j):
        return copy(quarter.at[k, (zl + j) % 4], got_z.at[k, j - 1], s_z, r_z.at[k], at_z(j))

    def ex_copy(k):
        return copy(ex_out.at[k], ex_in.at[k], s_ex, r_ex.at[k], other)

    def az_copy(k, j):
        here = act.at[k, y, zl]
        return copy(here, here, s_az, r_az.at[k], at_z(j))

    def ay_copy(k, side):
        here = act.at[k, y]
        return copy(here, here, s_ay, r_ay.at[k], at_y(1 + 2 * side))

    def af_copy(k, side):
        here = act.at[k, (y + 3 - 2 * side) % 4, pl.ds(2 * side, 2)]
        return copy(here, here, s_af, r_af.at[k], at_y(1 + 2 * side))

    def share_copy(k):
        dz, dx = chunk_dz(k), chunk_dx(k)
        return copy(share.at[k], got_x.at[dz, 3 - dx], s_share, r_share.at[dz], at_x(dx))

    def arrived(buffer, recv):
        copy(buffer, buffer, s_pair, recv, other).wait_recv()

    def left(buffer, send):
        copy(buffer, buffer, send, r_pair, other).wait_send()

    def first_conv(k):
        image = own if isinstance(k, int) else unpack(images[k], ROWS_A, keep)
        for tap in range(TAPS):
            moved = image
            if tap != 4:
                moved = pltpu.roll(image, shift_of(tap, sign), 1) * masks[tap]
            taps[k, pl.ds(ROWS_A * tap, ROWS_A), :] = moved
        total = jnp.dot(flipped[...], taps[k], preferred_element_type=F32)
        for block in range(4):
            piece = pack(total[80 * block : 80 * block + 80])
            for half in range(2):
                rows = piece[HALF * half : HALF * half + HALF]
                part_f[k, block, half] = rows
                part[k, block, half] = rows.astype(BF16)

    def send_parts(k):
        for half in range(2):
            relay_copy(k, half).start()
        for half in range(2):
            near_copy(k, half).start()

    def next_conv(k):
        @pl.when(k != FROM_PAIR)
        def _():
            arrived(images.at[k], r_img.at[k])

        first_conv(k)
        send_parts(k)

    def join(k):
        arrived(relayed.at[k], r_relay.at[k])
        for half in range(2):
            total = part_f[k, (y + 1 + 2 * half) % 4, half] + relayed[k, half].astype(F32)
            joined[k, half] = total.astype(BF16)
            join_copy(k, half).start()

    def sum_y(k):
        arrived(got_y.at[k], r_y.at[k])
        for half in range(2):
            total = part_f[k, y, half]
            for j in range(2):
                total = total + got_y[k, j, half].astype(F32)
            for side in range(2):
                piece = total[QUARTER * side : QUARTER * side + QUARTER]
                quarter_f[k, 2 * half + side] = piece
                quarter[k, 2 * half + side] = piece.astype(BF16)
        for j in (2, 3, 1):
            z_copy(k, j).start()

    def sum_z(k):
        arrived(got_z.at[k], r_z.at[k])
        total = quarter_f[k, zl]
        for j in range(3):
            total = total + got_z[k, j].astype(F32)
        pre[k] = total
        ex_out[k] = jnp.where(section == 0, silu(total), total).astype(BF16)
        ex_copy(k).start()

    def meet(k):
        arrived(ex_in.at[k], r_ex.at[k])
        incoming = ex_in[k].astype(F32)
        received = jnp.where(section == 0, incoming * silu_slope(pre[k]), incoming)
        act[k, y, zl] = received.astype(BF16)
        for j in (2, 3, 1):
            az_copy(k, j).start()

    def spread_y(k):
        arrived(got_z.at[k], r_az.at[k])
        for side in range(2):
            ay_copy(k, side).start()

    def forward_y(k):
        arrived(act.at[k, pl.ds(0, 2)], r_ay.at[k])
        for side in range(2):
            af_copy(k, side).start()

    def second_conv(k):
        arrived(act.at[k, 0], r_af.at[k])
        for block in range(4):
            piece = unpack(act[k, block].reshape(BLOCK_B, 128), 80, keep)
            act_all[k, pl.ds(80 * block, 80), :] = piece
        products[...] = jnp.dot(k_ref[...], act_all[k], preferred_element_type=F32)
        total = products[pl.ds(ROWS_A * 4, ROWS_A), :]
        for tap in range(TAPS):
            if tap != 4:
                moved = pltpu.roll(products[pl.ds(ROWS_A * tap, ROWS_A), :], shift_of(tap, -sign), 1)
                total = total + moved * masks_f[8 - tap]
        block = pack(total)
        if isinstance(k, int):
            own_sum[0] = block
            return
        dx = chunk_dx(k)

        @pl.when(dx == 0)
        def _():
            own_sum[chunk_dz(k)] = block

        @pl.when(dx != 0)
        def _():
            share[k] = block.astype(BF16)
            share_copy(k).start()

    def kernel_grad(k):
        grad_ref[...] += lax.dot_general(
            taps[k], act_all[k], (((1,), (1,)), ((), ())), preferred_element_type=F32
        )

    def sum_x(dz):
        arrived(got_x.at[dz], r_share.at[dz])
        total = own_sum[dz]
        for j in range(3):
            total = total + got_x[dz, j].astype(F32)
        return total

    stages = dict(
        next_conv=next_conv,
        join=join,
        sum_y=sum_y,
        sum_z=sum_z,
        meet=meet,
        spread_y=spread_y,
        forward_y=forward_y,
        second_conv=second_conv,
        kernel_grad=kernel_grad,
    )

    def step(t, carry):
        for when, j in ((1, 2), (5, 1)):

            @pl.when(t == when)
            def _():
                image_copy(0, 0, j).start()

        @pl.when(t == FROM_PAIR)
        def _():
            arrived(images.at[FROM_PAIR], r_img.at[FROM_PAIR])
            for j in (3, 2, 1):
                image_copy(FROM_PAIR, 1, j).start()

        for lag, first, stage in PLAN:

            @pl.when((t >= lag + first) & (t < CHUNKS + lag))
            def _():
                stages[stage](t - lag)

        return carry

    load.wait()
    flipped[...] = k_ref[...].T
    first_conv(0)
    pl.semaphore_wait(barrier, len(peers))
    to_pair.start()
    image_copy(0, 0, 3).start()
    send_parts(0)

    lax.fori_loop(1, CHUNKS + LAST, step, 0)

    across = copy(pair_out, pair_in, s_pair, r_pair, pair)
    pair_out[...] = sum_x(1).astype(BF16)
    across.start()
    second_conv(0)
    for k in LATE_GRADS:
        kernel_grad(k)
    total = sum_x(0)
    across.wait_recv()
    total = total + pair_in[...].astype(F32)
    out_ref[...] = unpack(total, ROWS_A, keep.astype(F32)).T[:PIXELS].astype(BF16)

    across.wait_send()
    left(images.at[pl.ds(0, 7)], s_img)
    left(relayed, s_relay)
    left(relayed, s_near)
    left(relayed, s_join)
    left(got_z, s_z)
    left(ex_out, s_ex)
    left(got_z, s_az)
    left(act.at[:, pl.ds(0, 2)], s_ay)
    left(act.at[:, 0], s_af)
    left(share.at[pl.ds(0, 6)], s_share)


def body(section_input, kernels):
    images, channels = section_input.shape[1], section_input.shape[4]
    inner = kernels.shape[4]
    scale = 1.0 / math.sqrt(CHUNKS * images * SIDE * SIDE)
    sem = pltpu.SemaphoreType.DMA
    pixels_first = section_input[0].transpose(1, 2, 0, 3).reshape(PIXELS, channels)
    out, grads = pl.pallas_call(
        kernel,
        out_shape=(
            jax.ShapeDtypeStruct((PIXELS, channels), BF16),
            pltpu.VMEM((TAPS * channels, inner), F32),
        ),
        in_specs=[pl.BlockSpec(memory_space=pltpu.VMEM), pl.BlockSpec(memory_space=pl.ANY)],
        out_specs=[pl.BlockSpec(memory_space=pltpu.VMEM)] * 2,
        scratch_shapes=[
            pltpu.VMEM((TAPS * channels, inner), BF16),
            pltpu.VMEM((TAPS, 1, LANES), BF16),
            pltpu.VMEM((TAPS, 1, LANES), F32),
            pltpu.VMEM((CHUNKS, BLOCK_A, 128), BF16),
            pltpu.VMEM((CHUNKS, TAPS * channels, LANES), BF16),
            pltpu.VMEM((inner, TAPS * channels), BF16),
            pltpu.VMEM((CHUNKS, 4, 2, HALF, 128), BF16),
            pltpu.VMEM((CHUNKS, 4, 2, HALF, 128), F32),
            pltpu.VMEM((CHUNKS, 2, HALF, 128), BF16),
            pltpu.VMEM((CHUNKS, 2, HALF, 128), BF16),
            pltpu.VMEM((CHUNKS, 2, 2, HALF, 128), BF16),
            pltpu.VMEM((CHUNKS, 4, QUARTER, 128), BF16),
            pltpu.VMEM((CHUNKS, 4, QUARTER, 128), F32),
            pltpu.VMEM((CHUNKS, 3, QUARTER, 128), BF16),
            pltpu.VMEM((CHUNKS, QUARTER, 128), F32),
            pltpu.VMEM((CHUNKS, QUARTER, 128), BF16),
            pltpu.VMEM((CHUNKS, QUARTER, 128), BF16),
            pltpu.VMEM((CHUNKS, 4, 4, QUARTER, 128), BF16),
            pltpu.VMEM((CHUNKS, inner, LANES), BF16),
            pltpu.VMEM((TAPS * channels, LANES), F32),
            pltpu.VMEM((CHUNKS, BLOCK_A, 128), BF16),
            pltpu.VMEM((2, 3, BLOCK_A, 128), BF16),
            pltpu.VMEM((2, BLOCK_A, 128), F32),
            pltpu.VMEM((BLOCK_A, 128), BF16),
            pltpu.VMEM((BLOCK_A, 128), BF16),
        ]
        + [sem] * 12
        + [sem((CHUNKS,))] * 8
        + [sem((2,)), sem],
        compiler_params=pltpu.CompilerParams(
            collective_id=0, has_side_effects=True, vmem_limit_bytes=60 * 2**20
        ),
        name="relay",
    )(pixels_first, kernels.reshape(TAPS * channels, inner))
    out = out.reshape(SIDE, SIDE, images, channels).transpose(2, 0, 1, 3)
    return out[None], (grads * scale).reshape(kernels.shape)


def solution(mesh):
    return jax.shard_map(
        body,
        mesh=mesh,
        in_specs=(
            P("section", "narrow", None, None, "wide"),
            P("section", None, None, "wide", "narrow"),
        ),
        out_specs=(
            P("section", "narrow", None, None, "wide"),
            P("section", None, None, "wide", "narrow"),
        ),
        check_vma=False,
    )
```

```python
import math

import jax
import jax.numpy as jnp
from jax import lax
from jax.experimental import pallas as pl
from jax.experimental.pallas import tpu as pltpu
from jax.sharding import PartitionSpec as P

MESH = pl.DeviceIdType.MESH
BF16 = jnp.bfloat16
F32 = jnp.float32

SIDE = 14
CHUNKS = 8
PIXELS = 2 * SIDE * SIDE
LANES = 512
SPILL = PIXELS - 384
TAPS = 9
ROWS_A = 160
ROWS_B = 320
BLOCK_A = 3 * ROWS_A + 16
BLOCK_B = 3 * (ROWS_B // 4) + 16
HALF = BLOCK_B // 2
QUARTER = BLOCK_B // 4

SLOT = {(0, 0): 0, (0, 1): 1, (0, 2): 2, (1, 0): 3, (1, 1): 4, (1, 2): 5, (1, 3): 6, (0, 3): 7}
FROM_PAIR = SLOT[(1, 0)]

SCHEDULE = (
    "A1", "J0", "A2", "R0", "J1", "A3", "Y0", "J2", "A7", "Y1", "J3", "A4", "Z0", "Y2", "A5", "M0", "A6",
    "Z1", "Y3", "J4", "Z2", "M1", "J5", "M2", "J6", "Y4", "Z3", "P1", "Y5", "P2", "Y6", "M3", "J7", "P0",
    "Z4", "M4", "Z5", "F2", "M5", "Z6", "F1", "P3", "M6", "Y7", "P4", "P5", "C1", "P6", "Z7", "F4", "M7",
    "F5", "F3", "F0", "C2", "F6", "G1", "C4", "P7", "C5", "C6", "G6", "F7", "C3", "G5", "G4", "X0", "G2",
    "C7", "C0", "G0", "G7", "G3", "W0",
)


def chunk_dz(k):
    return ((k + 1) // 4) % 2


def chunk_dx(k):
    late = k // 6
    return (1 - late) * (k % 3) + 3 * late


def silu(values):
    return values * jax.nn.sigmoid(values)


def silu_slope(values):
    logistic = jax.nn.sigmoid(values)
    return logistic * (1.0 + values * (1.0 - logistic))


def pack(values):
    rows = values.shape[0]
    spilled = values[:16, 384:]
    for group in range(1, rows // 16):
        spilled = spilled + pltpu.roll(values[16 * group : 16 * group + 16, 384:], SPILL * group, 1)
    return jnp.concatenate([values[:, 0:128], values[:, 128:256], values[:, 256:384], spilled], axis=0)


def unpack(block, rows, keep):
    spilled = block[3 * rows :]
    last = [spilled * keep]
    for group in range(1, rows // 16):
        last.append(pltpu.roll(spilled, 128 - SPILL * group, 1) * keep)
    parts = [block[0:rows], block[rows : 2 * rows], block[2 * rows : 3 * rows], jnp.concatenate(last, axis=0)]
    return jnp.concatenate(parts, axis=1)


def kernel(
    x_ref,
    k_hbm,
    out_ref,
    grad_ref,
    k_ref,
    masks,
    masks_f,
    images,
    taps,
    flipped,
    part,
    part_f,
    relayed,
    joined,
    got_y,
    quarter,
    quarter_f,
    got_z,
    pre,
    ex_out,
    ex_in,
    act,
    act_all,
    share,
    got_x,
    own_sum,
    pair_out,
    pair_in,
    turned,
    s_load,
    s_img,
    s_relay,
    s_near,
    s_join,
    s_z,
    s_ex,
    s_az,
    s_ay,
    s_af,
    s_share,
    s_pair,
    r_img,
    r_relay,
    r_y,
    r_z,
    r_ex,
    r_az,
    r_ay,
    r_af,
    r_share,
    r_pair,
):
    section = lax.axis_index("section")
    wide = lax.axis_index("wide")
    narrow = lax.axis_index("narrow")
    y, zl = wide // 4, wide % 4
    zh, x = narrow // 4, narrow % 4

    def at_y(j):
        return (section, ((y + j) % 4) * 4 + zl, narrow)

    def at_z(j):
        return (section, y * 4 + (zl + j) % 4, narrow)

    def at_x(j):
        return (section, wide, zh * 4 + (x + j) % 4)

    pair = (section, wide, (1 - zh) * 4 + x)
    other = (1 - section, wide, narrow)

    def copy(src, dst, send, recv, device):
        return pltpu.make_async_remote_copy(
            src_ref=src, dst_ref=dst, send_sem=send, recv_sem=recv, device_id=device, device_id_type=MESH
        )

    barrier = pltpu.get_barrier_semaphore()
    peers = [at_y(j) for j in (1, 3)] + [at_z(j) for j in (1, 2, 3)]
    peers += [at_x(j) for j in (1, 2, 3)] + [pair, other]
    for peer in peers:
        pl.semaphore_signal(barrier, inc=1, device_id=peer, device_id_type=MESH)

    load = pltpu.make_async_copy(k_hbm, k_ref, s_load)
    load.start()

    lane = lax.broadcasted_iota(jnp.int32, (1, LANES), 1)
    keep = (lane[:, :128] < SPILL).astype(BF16)

    def shift_of(tap, direction):
        offset = 2 * ((tap // 3 - 1) * SIDE + tap % 3 - 1)
        return (LANES - direction * offset) % LANES

    blank = jnp.zeros((LANES - PIXELS, ROWS_A), F32)
    own_f = jnp.concatenate([x_ref[...].astype(F32), blank], axis=0).T
    own = own_f.astype(BF16)
    images[0] = pack(own_f).astype(BF16)

    def image_copy(slot, dz, j):
        there = SLOT[(dz, (4 - j) % 4)]
        return copy(images.at[slot], images.at[there], s_img, r_img.at[there], at_x(j))

    to_pair = copy(images.at[0], images.at[FROM_PAIR], s_img, r_img.at[FROM_PAIR], pair)

    def relay_copy(k, half):
        return copy(
            part.at[k, (y + 2) % 4, half], relayed.at[k, half], s_relay, r_relay.at[k], at_y(1 + 2 * half)
        )

    def near_copy(k, half):
        j = 3 - 2 * half
        return copy(part.at[k, (y + j) % 4, half], got_y.at[k, 0, half], s_near, r_y.at[k], at_y(j))

    def join_copy(k, half):
        return copy(joined.at[k, half], got_y.at[k, 1, half], s_join, r_y.at[k], at_y(1 + 2 * half))

    def z_copy(k, j):
        return copy(quarter.at[k, (zl + j) % 4], got_z.at[k, j - 1], s_z, r_z.at[k], at_z(j))

    def ex_copy(k):
        return copy(ex_out.at[k], ex_in.at[k], s_ex, r_ex.at[k], other)

    def az_copy(k, j):
        here = act.at[k, y, zl]
        return copy(here, here, s_az, r_az.at[k], at_z(j))

    def ay_copy(k, side):
        here = act.at[k, y]
        return copy(here, here, s_ay, r_ay.at[k], at_y(1 + 2 * side))

    def af_copy(k, side):
        here = act.at[k, (y + 3 - 2 * side) % 4, pl.ds(2 * side, 2)]
        return copy(here, here, s_af, r_af.at[k], at_y(1 + 2 * side))

    def share_copy(k):
        dz, dx = chunk_dz(k), chunk_dx(k)
        return copy(share.at[k], got_x.at[dz, 3 - dx], s_share, r_share.at[dz], at_x(dx))

    def arrived(buffer, recv):
        copy(buffer, buffer, s_pair, recv, other).wait_recv()

    def left(buffer, send):
        copy(buffer, buffer, send, r_pair, other).wait_send()

    def first_conv(k):
        image = own if k == 0 else unpack(images[k], ROWS_A, keep)
        for tap in range(TAPS):
            moved = image
            if tap != 4:
                moved = pltpu.roll(image, shift_of(tap, sign), 1) * masks[tap]
            taps[k, pl.ds(ROWS_A * tap, ROWS_A), :] = moved
        total = jnp.dot(flipped[...], taps[k], preferred_element_type=F32)
        for block in range(4):
            piece = pack(total[80 * block : 80 * block + 80])
            for half in range(2):
                rows = piece[HALF * half : HALF * half + HALF]
                part_f[k, block, half] = rows
                part[k, block, half] = rows.astype(BF16)

    def send_parts(k):
        for half in range(2):
            relay_copy(k, half).start()
        for half in range(2):
            near_copy(k, half).start()

    def next_conv(k):
        if k != FROM_PAIR:
            arrived(images.at[k], r_img.at[k])

        first_conv(k)
        send_parts(k)

    def join(k):
        arrived(relayed.at[k], r_relay.at[k])
        for half in range(2):
            total = part_f[k, (y + 1 + 2 * half) % 4, half] + relayed[k, half].astype(F32)
            joined[k, half] = total.astype(BF16)
            join_copy(k, half).start()

    def sum_y(k):
        arrived(got_y.at[k], r_y.at[k])
        for half in range(2):
            total = part_f[k, y, half]
            for j in range(2):
                total = total + got_y[k, j, half].astype(F32)
            for side in range(2):
                piece = total[QUARTER * side : QUARTER * side + QUARTER]
                quarter_f[k, 2 * half + side] = piece
                quarter[k, 2 * half + side] = piece.astype(BF16)
        for j in (2, 3, 1):
            z_copy(k, j).start()

    def sum_z(k):
        arrived(got_z.at[k], r_z.at[k])
        total = quarter_f[k, zl]
        for j in range(3):
            total = total + got_z[k, j].astype(F32)
        pre[k] = total
        ex_out[k] = jnp.where(section == 0, silu(total), total).astype(BF16)
        ex_copy(k).start()

    def meet(k):
        arrived(ex_in.at[k], r_ex.at[k])
        incoming = ex_in[k].astype(F32)
        received = jnp.where(section == 0, incoming * silu_slope(pre[k]), incoming)
        act[k, y, zl] = received.astype(BF16)
        for j in (2, 3, 1):
            az_copy(k, j).start()

    def spread_y(k):
        arrived(got_z.at[k], r_az.at[k])
        for side in range(2):
            ay_copy(k, side).start()

    def forward_y(k):
        arrived(act.at[k, pl.ds(0, 2)], r_ay.at[k])
        for side in range(2):
            af_copy(k, side).start()

    def second_conv(k):
        arrived(act.at[k, 0], r_af.at[k])
        for block in range(4):
            piece = unpack(act[k, block].reshape(BLOCK_B, 128), 80, keep)
            act_all[k, pl.ds(80 * block, 80), :] = piece
        total = None
        for line in (1, 0, 2):
            rows = pl.ds(3 * ROWS_A * line, 3 * ROWS_A)
            product = jnp.dot(k_ref[rows], act_all[k], preferred_element_type=F32)
            for place in range(3):
                tap = 3 * line + place
                moved = product[ROWS_A * place : ROWS_A * place + ROWS_A]
                if tap != 4:
                    moved = pltpu.roll(moved, shift_of(tap, -sign), 1) * masks_f[8 - tap]
                total = moved if total is None else total + moved
        block = pack(total)
        dz, dx = chunk_dz(k), chunk_dx(k)
        if dx == 0:
            own_sum[dz] = block
        else:
            share[k] = block.astype(BF16)
            share_copy(k).start()

    def kernel_grad(k):
        turned[...] += lax.dot_general(
            act_all[k], taps[k], (((1,), (1,)), ((), ())), preferred_element_type=F32
        )

    def sum_x(dz):
        arrived(got_x.at[dz], r_share.at[dz])
        total = own_sum[dz]
        for j in range(3):
            total = total + got_x[dz, j].astype(F32)
        return total

    def pass_image(k):
        arrived(images.at[FROM_PAIR], r_img.at[FROM_PAIR])
        for j in (3, 2, 1):
            image_copy(FROM_PAIR, 1, j).start()

    across = copy(pair_out, pair_in, s_pair, r_pair, pair)

    def send_across(k):
        pair_out[...] = sum_x(1).astype(BF16)
        across.start()

    def finish(k):
        total = sum_x(0)
        across.wait_recv()
        total = total + pair_in[...].astype(F32)
        out_ref[...] = unpack(total, ROWS_A, keep.astype(F32)).T[:PIXELS].astype(BF16)

    stages = dict(
        A=next_conv,
        J=join,
        Y=sum_y,
        Z=sum_z,
        M=meet,
        P=spread_y,
        F=forward_y,
        C=second_conv,
        G=kernel_grad,
        R=pass_image,
        X=send_across,
        W=finish,
    )

    pl.semaphore_wait(barrier, len(peers))
    to_pair.start()
    image_copy(0, 0, 3).start()
    sign = 1 - 2 * section
    pixel = lane // 2
    row = pixel // SIDE
    column = pixel - SIDE * row
    for tap in range(TAPS):
        there_row = row + sign * (tap // 3 - 1)
        there_column = column + sign * (tap % 3 - 1)
        inside = (there_row >= 0) & (there_row < SIDE) & (there_column >= 0) & (there_column < SIDE)
        inside = (inside & (lane < PIXELS)).astype(F32)
        masks_f[tap] = inside
        masks[tap] = inside.astype(BF16)
    load.wait()
    flipped[...] = k_ref[...].T
    first_conv(0)
    send_parts(0)
    image_copy(0, 0, 2).start()
    image_copy(0, 0, 1).start()
    turned[...] = jnp.zeros_like(turned)

    for stage, k in SCHEDULE:
        stages[stage](int(k))

    grad_ref[...] = turned[...].T
    across.wait_send()
    left(images.at[pl.ds(0, 7)], s_img)
    left(relayed, s_relay)
    left(relayed, s_near)
    left(relayed, s_join)
    left(got_z, s_z)
    left(ex_out, s_ex)
    left(got_z, s_az)
    left(act.at[:, pl.ds(0, 2)], s_ay)
    left(act.at[:, 0], s_af)
    left(share.at[pl.ds(0, 6)], s_share)


def body(section_input, kernels):
    images, channels = section_input.shape[1], section_input.shape[4]
    inner = kernels.shape[4]
    scale = 1.0 / math.sqrt(CHUNKS * images * SIDE * SIDE)
    sem = pltpu.SemaphoreType.DMA
    pixels_first = section_input[0].transpose(1, 2, 0, 3).reshape(PIXELS, channels)
    out, grads = pl.pallas_call(
        kernel,
        out_shape=(
            jax.ShapeDtypeStruct((PIXELS, channels), BF16),
            pltpu.VMEM((TAPS * channels, inner), F32),
        ),
        in_specs=[pl.BlockSpec(memory_space=pltpu.VMEM), pl.BlockSpec(memory_space=pl.ANY)],
        out_specs=[pl.BlockSpec(memory_space=pltpu.VMEM)] * 2,
        scratch_shapes=[
            pltpu.VMEM((TAPS * channels, inner), BF16),
            pltpu.VMEM((TAPS, 1, LANES), BF16),
            pltpu.VMEM((TAPS, 1, LANES), F32),
            pltpu.VMEM((CHUNKS, BLOCK_A, 128), BF16),
            pltpu.VMEM((CHUNKS, TAPS * channels, LANES), BF16),
            pltpu.VMEM((inner, TAPS * channels), BF16),
            pltpu.VMEM((CHUNKS, 4, 2, HALF, 128), BF16),
            pltpu.VMEM((CHUNKS, 4, 2, HALF, 128), F32),
            pltpu.VMEM((CHUNKS, 2, HALF, 128), BF16),
            pltpu.VMEM((CHUNKS, 2, HALF, 128), BF16),
            pltpu.VMEM((CHUNKS, 2, 2, HALF, 128), BF16),
            pltpu.VMEM((CHUNKS, 4, QUARTER, 128), BF16),
            pltpu.VMEM((CHUNKS, 4, QUARTER, 128), F32),
            pltpu.VMEM((CHUNKS, 3, QUARTER, 128), BF16),
            pltpu.VMEM((CHUNKS, QUARTER, 128), F32),
            pltpu.VMEM((CHUNKS, QUARTER, 128), BF16),
            pltpu.VMEM((CHUNKS, QUARTER, 128), BF16),
            pltpu.VMEM((CHUNKS, 4, 4, QUARTER, 128), BF16),
            pltpu.VMEM((CHUNKS, inner, LANES), BF16),
            pltpu.VMEM((CHUNKS, BLOCK_A, 128), BF16),
            pltpu.VMEM((2, 3, BLOCK_A, 128), BF16),
            pltpu.VMEM((2, BLOCK_A, 128), F32),
            pltpu.VMEM((BLOCK_A, 128), BF16),
            pltpu.VMEM((BLOCK_A, 128), BF16),
            pltpu.VMEM((inner, TAPS * channels), F32),
        ]
        + [sem] * 12
        + [sem((CHUNKS,))] * 8
        + [sem((2,)), sem],
        compiler_params=pltpu.CompilerParams(
            collective_id=0, has_side_effects=True, vmem_limit_bytes=60 * 2**20
        ),
        name="relay",
    )(pixels_first, kernels.reshape(TAPS * channels, inner))
    out = out.reshape(SIDE, SIDE, images, channels).transpose(2, 0, 1, 3)
    return out[None], (grads * scale).reshape(kernels.shape)


def solution(mesh):
    return jax.shard_map(
        body,
        mesh=mesh,
        in_specs=(
            P("section", "narrow", None, None, "wide"),
            P("section", None, None, "wide", "narrow"),
        ),
        out_specs=(
            P("section", "narrow", None, None, "wide"),
            P("section", None, None, "wide", "narrow"),
        ),
        check_vma=False,
    )
```

```python
import functools
import math

import jax
import jax.numpy as jnp
from jax import lax
from jax.experimental import pallas as pl
from jax.experimental.pallas import tpu as pltpu
from jax.sharding import PartitionSpec as P

MESH = pl.DeviceIdType.MESH
BF16 = jnp.bfloat16
F32 = jnp.float32

SIDE = 14
CHUNKS = 8
PIXELS = 2 * SIDE * SIDE
LANES = 512
SPILL = PIXELS - 384
TAPS = 9
ROWS_A = 160
ROWS_B = 320
BLOCK_A = 3 * ROWS_A + 16
BLOCK_B = 3 * (ROWS_B // 4) + 16
HALF = BLOCK_B // 2
QUARTER = BLOCK_B // 4

SLOT = {(0, 0): 0, (0, 1): 1, (0, 2): 2, (1, 0): 3, (1, 1): 4, (1, 2): 5, (1, 3): 6, (0, 3): 7}
FROM_PAIR = SLOT[(1, 0)]

STRAIGHT_SUMS = (0, 1, 3)
STRAIGHT_GATHERS = (5, 6, 7)

SCHEDULE = (
    "A1", "R0", "A3", "Y0", "A7", "Y1", "A4", "A5", "Y3", "A6", "Z1", "Z0", "M1", "J4", "J7", "M0", "J5",
    "Z3", "A2", "M3", "J6", "Y4", "P1", "Y5", "J2", "Y6", "P3", "Y7", "Z4", "M4", "Z5", "F1", "P0", "M5",
    "Y2", "Z6", "F3", "M6", "P4", "Z7", "M7", "P5", "Z2", "M2", "F4", "P6", "C3", "G3", "C5", "P2", "P7",
    "F0", "C4", "C6", "G4", "F2", "G5", "C1", "C7", "X0", "C2", "G1", "G7", "C0", "G2", "G0", "G6", "W0",
)


def chunk_dz(k):
    return ((k + 1) // 4) % 2


def chunk_dx(k):
    late = k // 6
    return (1 - late) * (k % 3) + 3 * late


def silu(values):
    return values * jax.nn.sigmoid(values)


def silu_slope(values):
    logistic = jax.nn.sigmoid(values)
    return logistic * (1.0 + values * (1.0 - logistic))


def pack(values):
    rows = values.shape[0]
    spilled = values[:16, 384:]
    for group in range(1, rows // 16):
        spilled = spilled + pltpu.roll(values[16 * group : 16 * group + 16, 384:], SPILL * group, 1)
    return jnp.concatenate([values[:, 0:128], values[:, 128:256], values[:, 256:384], spilled], axis=0)


def unpack(block, rows, keep):
    spilled = block[3 * rows :]
    last = [spilled * keep]
    for group in range(1, rows // 16):
        last.append(pltpu.roll(spilled, 128 - SPILL * group, 1) * keep)
    parts = [block[0:rows], block[rows : 2 * rows], block[2 * rows : 3 * rows], jnp.concatenate(last, axis=0)]
    return jnp.concatenate(parts, axis=1)


def kernel(
    scale,
    x_ref,
    k_hbm,
    out_ref,
    grad_ref,
    k_ref,
    masks,
    masks_f,
    images,
    taps,
    flipped,
    part,
    part_f,
    relayed,
    joined,
    got_y,
    quarter,
    quarter_f,
    got_z,
    pre,
    ex_out,
    ex_in,
    act,
    act_all,
    share,
    got_x,
    own_sum,
    pair_out,
    pair_in,
    turned,
    s_load,
    s_img,
    s_relay,
    s_near,
    s_join,
    s_z,
    s_ex,
    s_az,
    s_ay,
    s_af,
    s_share,
    s_straight,
    s_gather,
    s_pair,
    r_img,
    r_relay,
    r_y,
    r_z,
    r_ex,
    r_az,
    r_ay,
    r_af,
    r_share,
    r_pair,
):
    section = lax.axis_index("section")
    wide = lax.axis_index("wide")
    narrow = lax.axis_index("narrow")
    y, zl = wide // 4, wide % 4
    zh, x = narrow // 4, narrow % 4

    def at_y(j):
        return (section, ((y + j) % 4) * 4 + zl, narrow)

    def at_z(j):
        return (section, y * 4 + (zl + j) % 4, narrow)

    def at_x(j):
        return (section, wide, zh * 4 + (x + j) % 4)

    pair = (section, wide, (1 - zh) * 4 + x)
    other = (1 - section, wide, narrow)

    def copy(src, dst, send, recv, device):
        return pltpu.make_async_remote_copy(
            src_ref=src, dst_ref=dst, send_sem=send, recv_sem=recv, device_id=device, device_id_type=MESH
        )

    barrier = pltpu.get_barrier_semaphore()
    peers = [at_y(j) for j in (1, 2, 3)] + [at_z(j) for j in (1, 2, 3)]
    peers += [at_x(j) for j in (1, 2, 3)] + [pair, other]
    for peer in peers:
        pl.semaphore_signal(barrier, inc=1, device_id=peer, device_id_type=MESH)

    load = pltpu.make_async_copy(k_hbm, k_ref, s_load)
    load.start()

    lane = lax.broadcasted_iota(jnp.int32, (1, LANES), 1)
    keep = (lane[:, :128] < SPILL).astype(BF16)

    def shift_of(tap, direction):
        offset = 2 * ((tap // 3 - 1) * SIDE + tap % 3 - 1)
        return (LANES - direction * offset) % LANES

    blank = jnp.zeros((LANES - PIXELS, ROWS_A), F32)
    own_f = jnp.concatenate([x_ref[...].reshape(PIXELS, ROWS_A).astype(F32), blank], axis=0).T
    own = own_f.astype(BF16)
    images[0] = pack(own_f).astype(BF16)

    def image_copy(slot, dz, j):
        there = SLOT[(dz, (4 - j) % 4)]
        return copy(images.at[slot], images.at[there], s_img, r_img.at[there], at_x(j))

    to_pair = copy(images.at[0], images.at[FROM_PAIR], s_img, r_img.at[FROM_PAIR], pair)

    def relay_copy(k, half):
        return copy(
            part.at[k, (y + 2) % 4, half], relayed.at[k, half], s_relay, r_relay.at[k], at_y(1 + 2 * half)
        )

    def near_copy(k, half):
        j = 3 - 2 * half
        return copy(part.at[k, (y + j) % 4, half], got_y.at[k, 0, half], s_near, r_y.at[k], at_y(j))

    def straight_copy(k, j):
        return copy(part.at[k, (y + j) % 4], got_y.at[k, j - 1], s_straight, r_y.at[k], at_y(j))

    def gather_copy(k, j):
        here = act.at[k, y]
        return copy(here, here, s_gather, r_ay.at[k], at_y(j))

    def join_copy(k, half):
        return copy(joined.at[k, half], got_y.at[k, 1, half], s_join, r_y.at[k], at_y(1 + 2 * half))

    def z_copy(k, j):
        return copy(quarter.at[k, (zl + j) % 4], got_z.at[k, j - 1], s_z, r_z.at[k], at_z(j))

    def ex_copy(k):
        return copy(ex_out.at[k], ex_in.at[k], s_ex, r_ex.at[k], other)

    def az_copy(k, j):
        here = act.at[k, y, zl]
        return copy(here, here, s_az, r_az.at[k], at_z(j))

    def ay_copy(k, side):
        here = act.at[k, y]
        return copy(here, here, s_ay, r_ay.at[k], at_y(1 + 2 * side))

    def af_copy(k, side):
        here = act.at[k, (y + 3 - 2 * side) % 4, pl.ds(2 * side, 2)]
        return copy(here, here, s_af, r_af.at[k], at_y(1 + 2 * side))

    def share_copy(k):
        dz, dx = chunk_dz(k), chunk_dx(k)
        return copy(share.at[k], got_x.at[dz, 3 - dx], s_share, r_share.at[dz], at_x(dx))

    def arrived(buffer, recv):
        copy(buffer, buffer, s_pair, recv, other).wait_recv()

    def left(buffer, send):
        copy(buffer, buffer, send, r_pair, other).wait_send()

    def first_conv(k):
        image = own if k == 0 else unpack(images[k], ROWS_A, keep)
        for tap in range(TAPS):
            moved = image
            if tap != 4:
                moved = pltpu.roll(image, shift_of(tap, sign), 1) * masks[tap]
            taps[k, pl.ds(ROWS_A * tap, ROWS_A), :] = moved
        total = jnp.dot(flipped[...], taps[k], preferred_element_type=F32)
        for block in range(4):
            piece = pack(total[80 * block : 80 * block + 80])
            for half in range(2):
                rows = piece[HALF * half : HALF * half + HALF]
                part_f[k, block, half] = rows
                part[k, block, half] = rows.astype(BF16)

    def send_parts(k):
        if k in STRAIGHT_SUMS:
            for j in (2, 1, 3):
                straight_copy(k, j).start()
            return
        for half in range(2):
            relay_copy(k, half).start()
        for half in range(2):
            near_copy(k, half).start()

    def next_conv(k):
        if k != FROM_PAIR:
            arrived(images.at[k], r_img.at[k])

        first_conv(k)
        send_parts(k)

    def join(k):
        arrived(relayed.at[k], r_relay.at[k])
        for half in range(2):
            total = part_f[k, (y + 1 + 2 * half) % 4, half] + relayed[k, half].astype(F32)
            joined[k, half] = total.astype(BF16)
            join_copy(k, half).start()

    def sum_y(k):
        pieces = 3 if k in STRAIGHT_SUMS else 2
        arrived(got_y.at[k, pl.ds(0, pieces)], r_y.at[k])
        for half in range(2):
            total = part_f[k, y, half]
            for j in range(pieces):
                total = total + got_y[k, j, half].astype(F32)
            for side in range(2):
                piece = total[QUARTER * side : QUARTER * side + QUARTER]
                quarter_f[k, 2 * half + side] = piece
                quarter[k, 2 * half + side] = piece.astype(BF16)
        for j in (2, 3, 1):
            z_copy(k, j).start()

    def sum_z(k):
        arrived(got_z.at[k], r_z.at[k])
        total = quarter_f[k, zl]
        for j in range(3):
            total = total + got_z[k, j].astype(F32)
        pre[k] = total
        ex_out[k] = jnp.where(section == 0, silu(total), total).astype(BF16)
        ex_copy(k).start()

    def meet(k):
        arrived(ex_in.at[k], r_ex.at[k])
        incoming = ex_in[k].astype(F32)
        received = jnp.where(section == 0, incoming * silu_slope(pre[k]), incoming)
        act[k, y, zl] = received.astype(BF16)
        for j in (2, 3, 1):
            az_copy(k, j).start()

    def spread_y(k):
        arrived(got_z.at[k], r_az.at[k])
        if k in STRAIGHT_GATHERS:
            for j in (2, 1, 3):
                gather_copy(k, j).start()
            return
        for side in range(2):
            ay_copy(k, side).start()

    def forward_y(k):
        arrived(act.at[k, pl.ds(0, 2)], r_ay.at[k])
        for side in range(2):
            af_copy(k, side).start()

    def second_conv(k):
        if k in STRAIGHT_GATHERS:
            arrived(act.at[k, pl.ds(0, 3)], r_ay.at[k])
        else:
            arrived(act.at[k, 0], r_af.at[k])
        for block in range(4):
            piece = unpack(act[k, block].reshape(BLOCK_B, 128), 80, keep)
            act_all[k, pl.ds(80 * block, 80), :] = piece
        total = None
        for line in (1, 0, 2):
            rows = pl.ds(3 * ROWS_A * line, 3 * ROWS_A)
            product = jnp.dot(k_ref[rows], act_all[k], preferred_element_type=F32)
            for place in range(3):
                tap = 3 * line + place
                moved = product[ROWS_A * place : ROWS_A * place + ROWS_A]
                if tap != 4:
                    moved = pltpu.roll(moved, shift_of(tap, -sign), 1) * masks_f[8 - tap]
                total = moved if total is None else total + moved
        block = pack(total)
        dz, dx = chunk_dz(k), chunk_dx(k)
        if dx == 0:
            own_sum[dz] = block
        else:
            share[k] = block.astype(BF16)
            share_copy(k).start()

    def kernel_grad(k):
        turned[...] += lax.dot_general(
            act_all[k], taps[k], (((1,), (1,)), ((), ())), preferred_element_type=F32
        )

    def sum_x(dz):
        arrived(got_x.at[dz], r_share.at[dz])
        total = own_sum[dz]
        for j in range(3):
            total = total + got_x[dz, j].astype(F32)
        return total

    def pass_image(k):
        arrived(images.at[FROM_PAIR], r_img.at[FROM_PAIR])
        for j in (3, 2, 1):
            image_copy(FROM_PAIR, 1, j).start()

    across = copy(pair_out, pair_in, s_pair, r_pair, pair)

    def send_across(k):
        pair_out[...] = sum_x(1).astype(BF16)
        across.start()

    def finish(k):
        grad_ref[...] = turned[...].T * scale
        total = sum_x(0)
        across.wait_recv()
        total = total + pair_in[...].astype(F32)
        total = unpack(total, ROWS_A, keep.astype(F32)).T[:PIXELS].astype(BF16)
        out_ref[...] = total.reshape(out_ref.shape)

    stages = dict(
        A=next_conv,
        J=join,
        Y=sum_y,
        Z=sum_z,
        M=meet,
        P=spread_y,
        F=forward_y,
        C=second_conv,
        G=kernel_grad,
        R=pass_image,
        X=send_across,
        W=finish,
    )

    pl.semaphore_wait(barrier, len(peers))
    to_pair.start()
    image_copy(0, 0, 3).start()
    sign = 1 - 2 * section
    pixel = lane // 2
    row = pixel // SIDE
    column = pixel - SIDE * row
    for tap in range(TAPS):
        there_row = row + sign * (tap // 3 - 1)
        there_column = column + sign * (tap % 3 - 1)
        inside = (there_row >= 0) & (there_row < SIDE) & (there_column >= 0) & (there_column < SIDE)
        inside = (inside & (lane < PIXELS)).astype(F32)
        masks_f[tap] = inside
        masks[tap] = inside.astype(BF16)
    load.wait()
    flipped[...] = k_ref[...].T
    first_conv(0)
    send_parts(0)
    image_copy(0, 0, 2).start()
    image_copy(0, 0, 1).start()
    turned[...] = jnp.zeros_like(turned)

    for stage, k in SCHEDULE:
        stages[stage](int(k))

    across.wait_send()
    left(images.at[pl.ds(0, 7)], s_img)
    round_sums = CHUNKS - len(STRAIGHT_SUMS)
    round_gathers = CHUNKS - len(STRAIGHT_GATHERS)
    for send in (s_relay, s_near, s_join):
        left(relayed.at[pl.ds(0, round_sums)], send)
    left(act.at[pl.ds(0, round_gathers), pl.ds(0, 2)], s_ay)
    left(act.at[pl.ds(0, round_gathers), 0], s_af)
    if STRAIGHT_SUMS:
        left(got_y.at[pl.ds(0, len(STRAIGHT_SUMS))], s_straight)
    if STRAIGHT_GATHERS:
        left(act.at[pl.ds(0, len(STRAIGHT_GATHERS)), pl.ds(0, 3)], s_gather)
    left(got_z, s_z)
    left(ex_out, s_ex)
    left(got_z, s_az)
    left(share.at[pl.ds(0, 6)], s_share)


def body(section_input, kernels):
    images, channels = section_input.shape[1], section_input.shape[4]
    inner = kernels.shape[4]
    scale = 1.0 / math.sqrt(CHUNKS * images * SIDE * SIDE)
    sem = pltpu.SemaphoreType.DMA
    pixels_first = section_input[0].transpose(1, 2, 0, 3).reshape(SIDE * SIDE, images, channels)
    out, grads = pl.pallas_call(
        functools.partial(kernel, scale),
        out_shape=(
            jax.ShapeDtypeStruct((SIDE * SIDE, images, channels), BF16),
            pltpu.VMEM((TAPS * channels, inner), F32),
        ),
        in_specs=[pl.BlockSpec(memory_space=pltpu.VMEM), pl.BlockSpec(memory_space=pl.ANY)],
        out_specs=[pl.BlockSpec(memory_space=pltpu.VMEM)] * 2,
        scratch_shapes=[
            pltpu.VMEM((TAPS * channels, inner), BF16),
            pltpu.VMEM((TAPS, 1, LANES), BF16),
            pltpu.VMEM((TAPS, 1, LANES), F32),
            pltpu.VMEM((CHUNKS, BLOCK_A, 128), BF16),
            pltpu.VMEM((CHUNKS, TAPS * channels, LANES), BF16),
            pltpu.VMEM((inner, TAPS * channels), BF16),
            pltpu.VMEM((CHUNKS, 4, 2, HALF, 128), BF16),
            pltpu.VMEM((CHUNKS, 4, 2, HALF, 128), F32),
            pltpu.VMEM((CHUNKS, 2, HALF, 128), BF16),
            pltpu.VMEM((CHUNKS, 2, HALF, 128), BF16),
            pltpu.VMEM((CHUNKS, 3, 2, HALF, 128), BF16),
            pltpu.VMEM((CHUNKS, 4, QUARTER, 128), BF16),
            pltpu.VMEM((CHUNKS, 4, QUARTER, 128), F32),
            pltpu.VMEM((CHUNKS, 3, QUARTER, 128), BF16),
            pltpu.VMEM((CHUNKS, QUARTER, 128), F32),
            pltpu.VMEM((CHUNKS, QUARTER, 128), BF16),
            pltpu.VMEM((CHUNKS, QUARTER, 128), BF16),
            pltpu.VMEM((CHUNKS, 4, 4, QUARTER, 128), BF16),
            pltpu.VMEM((CHUNKS, inner, LANES), BF16),
            pltpu.VMEM((CHUNKS, BLOCK_A, 128), BF16),
            pltpu.VMEM((2, 3, BLOCK_A, 128), BF16),
            pltpu.VMEM((2, BLOCK_A, 128), F32),
            pltpu.VMEM((BLOCK_A, 128), BF16),
            pltpu.VMEM((BLOCK_A, 128), BF16),
            pltpu.VMEM((inner, TAPS * channels), F32),
        ]
        + [sem] * 14
        + [sem((CHUNKS,))] * 8
        + [sem((2,)), sem],
        compiler_params=pltpu.CompilerParams(
            collective_id=0, has_side_effects=True, vmem_limit_bytes=60 * 2**20
        ),
        name="relay",
    )(pixels_first, kernels.reshape(TAPS * channels, inner))
    out = out.reshape(SIDE, SIDE, images, channels).transpose(2, 0, 1, 3)
    return out[None], grads.reshape(kernels.shape)


def solution(mesh):
    return jax.shard_map(
        body,
        mesh=mesh,
        in_specs=(
            P("section", "narrow", None, None, "wide"),
            P("section", None, None, "wide", "narrow"),
        ),
        out_specs=(
            P("section", "narrow", None, None, "wide"),
            P("section", None, None, "wide", "narrow"),
        ),
        check_vma=False,
    )
```

```python
import functools
import math

import jax
import jax.numpy as jnp
from jax import lax
from jax.experimental import pallas as pl
from jax.experimental.pallas import tpu as pltpu
from jax.sharding import PartitionSpec as P

MESH = pl.DeviceIdType.MESH
BF16 = jnp.bfloat16
F32 = jnp.float32

SIDE = 14
CHUNKS = 8
PIXELS = 2 * SIDE * SIDE
LANES = 512
SPILL = PIXELS - 384
TAPS = 9
ROWS_A = 160
ROWS_B = 320
BLOCK_A = 3 * ROWS_A + 16
BLOCK_B = 3 * (ROWS_B // 4) + 16
HALF = BLOCK_B // 2
QUARTER = BLOCK_B // 4

SLOT = {(0, 0): 0, (0, 1): 1, (0, 2): 2, (1, 0): 3, (1, 1): 4, (1, 2): 5, (1, 3): 6, (0, 3): 7}
FROM_PAIR = SLOT[(1, 0)]

STRAIGHT_SUMS = (0, 1, 3, 4)
STRAIGHT_GATHERS = (4, 5, 6, 7)

SCHEDULE = (
    "A1", "R0", "R1", "A3", "Y0", "A4", "Y1", "A6", "Z0", "Y3", "A5", "M0", "A2", "Z1", "Y4", "M1", "J6",
    "A7", "J5", "Z3", "M3", "P0", "Z4", "J2", "Y6", "M4", "J7", "P1", "Y5", "P3", "Y2", "Z6", "M6", "P4",
    "Y7", "Z5", "Z2", "M5", "F3", "F1", "M2", "P6", "Z7", "C4", "P5", "M7", "C1", "P2", "G4", "C6", "P7",
    "C5", "F0", "G5", "F2", "C3", "G3", "C7", "X0", "G7", "C2", "C0", "G2", "G0", "G1", "G6", "W0",
)


def chunk_dz(k):
    return ((k + 1) // 4) % 2


def chunk_dx(k):
    late = k // 6
    return (1 - late) * (k % 3) + 3 * late


def silu(values):
    return values * jax.nn.sigmoid(values)


def silu_slope(values):
    logistic = jax.nn.sigmoid(values)
    return logistic * (1.0 + values * (1.0 - logistic))


def pack(values):
    rows = values.shape[0]
    spilled = values[:16, 384:]
    for group in range(1, rows // 16):
        spilled = spilled + pltpu.roll(values[16 * group : 16 * group + 16, 384:], SPILL * group, 1)
    return jnp.concatenate([values[:, 0:128], values[:, 128:256], values[:, 256:384], spilled], axis=0)


def unpack(block, rows, keep):
    spilled = block[3 * rows :]
    last = [spilled * keep]
    for group in range(1, rows // 16):
        last.append(pltpu.roll(spilled, 128 - SPILL * group, 1) * keep)
    parts = [block[0:rows], block[rows : 2 * rows], block[2 * rows : 3 * rows], jnp.concatenate(last, axis=0)]
    return jnp.concatenate(parts, axis=1)


def kernel(
    scale,
    x_hbm,
    k_hbm,
    out_ref,
    grad_ref,
    x_ref,
    k_ref,
    masks,
    masks_f,
    images,
    taps,
    flipped,
    part,
    part_f,
    relayed,
    joined,
    got_y,
    quarter,
    quarter_f,
    got_z,
    pre,
    ex_out,
    ex_in,
    act,
    act_all,
    share,
    got_x,
    own_sum,
    pair_out,
    pair_in,
    turned,
    s_load_x,
    s_load,
    s_img,
    s_relay,
    s_near,
    s_join,
    s_z,
    s_ex,
    s_az,
    s_ay,
    s_af,
    s_share,
    s_straight,
    s_gather,
    s_pair,
    r_pair_img,
    r_img,
    r_relay,
    r_y,
    r_z,
    r_ex,
    r_az,
    r_ay,
    r_af,
    r_share,
    r_pair,
):
    section = lax.axis_index("section")
    wide = lax.axis_index("wide")
    narrow = lax.axis_index("narrow")
    y, zl = wide // 4, wide % 4
    zh, x = narrow // 4, narrow % 4

    def at_y(j):
        return (section, ((y + j) % 4) * 4 + zl, narrow)

    def at_z(j):
        return (section, y * 4 + (zl + j) % 4, narrow)

    def at_x(j):
        return (section, wide, zh * 4 + (x + j) % 4)

    pair = (section, wide, (1 - zh) * 4 + x)
    other = (1 - section, wide, narrow)

    def copy(src, dst, send, recv, device):
        return pltpu.make_async_remote_copy(
            src_ref=src, dst_ref=dst, send_sem=send, recv_sem=recv, device_id=device, device_id_type=MESH
        )

    barrier = pltpu.get_barrier_semaphore()
    peers = [pair] + [at_z(j) for j in (2, 1, 3)] + [at_x(j) for j in (2, 1, 3)]
    peers += [at_y(j) for j in (2, 1, 3)] + [other]
    for peer in peers:
        pl.semaphore_signal(barrier, inc=1, device_id=peer, device_id_type=MESH)

    load_x = pltpu.make_async_copy(x_hbm, x_ref, s_load_x)
    load_x.start()
    load = pltpu.make_async_copy(k_hbm, k_ref, s_load)
    load.start()

    lane = lax.broadcasted_iota(jnp.int32, (1, LANES), 1)
    keep = (lane[:, :128] < SPILL).astype(BF16)

    def shift_of(tap, direction):
        offset = 2 * ((tap // 3 - 1) * SIDE + tap % 3 - 1)
        return (LANES - direction * offset) % LANES

    blank = jnp.zeros((LANES - PIXELS, ROWS_A), F32)
    load_x.wait()
    own_f = jnp.concatenate([x_ref[...].reshape(PIXELS, ROWS_A).astype(F32), blank], axis=0).T
    own = own_f.astype(BF16)
    images[0] = pack(own_f).astype(BF16)

    def image_copy(j):
        there = SLOT[(0, (4 - j) % 4)]
        return copy(images.at[0], images.at[there], s_img, r_img.at[there], at_x(j))

    pieces_of_image = (pl.ds(0, 256), pl.ds(256, BLOCK_A - 256))

    def pair_copy(piece):
        rows = pieces_of_image[piece]
        there = images.at[FROM_PAIR, rows]
        return copy(images.at[0, rows], there, s_img, r_pair_img.at[piece], pair)

    def pass_copy(piece, j):
        rows = pieces_of_image[piece]
        slot = SLOT[(1, (4 - j) % 4)]
        return copy(images.at[FROM_PAIR, rows], images.at[slot, rows], s_img, r_img.at[slot], at_x(j))

    def relay_copy(k, half):
        return copy(
            part.at[k, (y + 2) % 4, half], relayed.at[k, half], s_relay, r_relay.at[k], at_y(1 + 2 * half)
        )

    def near_copy(k, half):
        j = 3 - 2 * half
        return copy(part.at[k, (y + j) % 4, half], got_y.at[k, 0, half], s_near, r_y.at[k], at_y(j))

    def straight_copy(k, j):
        return copy(part.at[k, (y + j) % 4], got_y.at[k, j - 1], s_straight, r_y.at[k], at_y(j))

    def gather_copy(k, j):
        here = act.at[k, y]
        return copy(here, here, s_gather, r_ay.at[k], at_y(j))

    def join_copy(k, half):
        return copy(joined.at[k, half], got_y.at[k, 1, half], s_join, r_y.at[k], at_y(1 + 2 * half))

    def z_copy(k, j):
        return copy(quarter.at[k, (zl + j) % 4], got_z.at[k, j - 1], s_z, r_z.at[k], at_z(j))

    def ex_copy(k):
        return copy(ex_out.at[k], ex_in.at[k], s_ex, r_ex.at[k], other)

    def az_copy(k, j):
        here = act.at[k, y, zl]
        return copy(here, here, s_az, r_az.at[k], at_z(j))

    def ay_copy(k, side):
        here = act.at[k, y]
        return copy(here, here, s_ay, r_ay.at[k], at_y(1 + 2 * side))

    def af_copy(k, side):
        here = act.at[k, (y + 3 - 2 * side) % 4, pl.ds(2 * side, 2)]
        return copy(here, here, s_af, r_af.at[k], at_y(1 + 2 * side))

    def share_copy(k):
        dz, dx = chunk_dz(k), chunk_dx(k)
        return copy(share.at[k], got_x.at[dz, 3 - dx], s_share, r_share.at[dz], at_x(dx))

    def arrived(buffer, recv):
        copy(buffer, buffer, s_pair, recv, other).wait_recv()

    def left(buffer, send):
        copy(buffer, buffer, send, r_pair, other).wait_send()

    def first_conv(k):
        image = own if k == 0 else unpack(images[k], ROWS_A, keep)
        for tap in range(TAPS):
            moved = image
            if tap != 4:
                moved = pltpu.roll(image, shift_of(tap, sign), 1) * masks[tap]
            taps[k, pl.ds(ROWS_A * tap, ROWS_A), :] = moved
        total = jnp.dot(flipped[...], taps[k], preferred_element_type=F32)
        for block in range(4):
            piece = pack(total[80 * block : 80 * block + 80])
            for half in range(2):
                rows = piece[HALF * half : HALF * half + HALF]
                part_f[k, block, half] = rows
                part[k, block, half] = rows.astype(BF16)

    def send_parts(k):
        if k in STRAIGHT_SUMS:
            for j in (2, 1, 3):
                straight_copy(k, j).start()
            return
        for half in range(2):
            relay_copy(k, half).start()
        for half in range(2):
            near_copy(k, half).start()

    def next_conv(k):
        if k != FROM_PAIR:
            arrived(images.at[k], r_img.at[k])

        first_conv(k)
        send_parts(k)

    def join(k):
        arrived(relayed.at[k], r_relay.at[k])
        for half in range(2):
            total = part_f[k, (y + 1 + 2 * half) % 4, half] + relayed[k, half].astype(F32)
            joined[k, half] = total.astype(BF16)
            join_copy(k, half).start()

    def sum_y(k):
        pieces = 3 if k in STRAIGHT_SUMS else 2
        arrived(got_y.at[k, pl.ds(0, pieces)], r_y.at[k])
        for half in range(2):
            total = part_f[k, y, half]
            for j in range(pieces):
                total = total + got_y[k, j, half].astype(F32)
            for side in range(2):
                piece = total[QUARTER * side : QUARTER * side + QUARTER]
                quarter_f[k, 2 * half + side] = piece
                quarter[k, 2 * half + side] = piece.astype(BF16)
        for j in (2, 3, 1):
            z_copy(k, j).start()

    def sum_z(k):
        arrived(got_z.at[k], r_z.at[k])
        total = quarter_f[k, zl]
        for j in range(3):
            total = total + got_z[k, j].astype(F32)
        pre[k] = total
        ex_out[k] = jnp.where(section == 0, silu(total), total).astype(BF16)
        ex_copy(k).start()

    def meet(k):
        arrived(ex_in.at[k], r_ex.at[k])
        incoming = ex_in[k].astype(F32)
        received = jnp.where(section == 0, incoming * silu_slope(pre[k]), incoming)
        act[k, y, zl] = received.astype(BF16)
        for j in (2, 3, 1):
            az_copy(k, j).start()

    def spread_y(k):
        arrived(got_z.at[k], r_az.at[k])
        if k in STRAIGHT_GATHERS:
            for j in (2, 1, 3):
                gather_copy(k, j).start()
            return
        for side in range(2):
            ay_copy(k, side).start()

    def forward_y(k):
        arrived(act.at[k, pl.ds(0, 2)], r_ay.at[k])
        for side in range(2):
            af_copy(k, side).start()

    def second_conv(k):
        if k in STRAIGHT_GATHERS:
            arrived(act.at[k, pl.ds(0, 3)], r_ay.at[k])
        else:
            arrived(act.at[k, 0], r_af.at[k])
        for block in range(4):
            piece = unpack(act[k, block].reshape(BLOCK_B, 128), 80, keep)
            act_all[k, pl.ds(80 * block, 80), :] = piece
        total = None
        for line in (1, 0, 2):
            rows = pl.ds(3 * ROWS_A * line, 3 * ROWS_A)
            product = jnp.dot(k_ref[rows], act_all[k], preferred_element_type=F32)
            for place in range(3):
                tap = 3 * line + place
                moved = product[ROWS_A * place : ROWS_A * place + ROWS_A]
                if tap != 4:
                    moved = pltpu.roll(moved, shift_of(tap, -sign), 1) * masks_f[8 - tap]
                total = moved if total is None else total + moved
        block = pack(total)
        dz, dx = chunk_dz(k), chunk_dx(k)
        if dx == 0:
            own_sum[dz] = block
        else:
            share[k] = block.astype(BF16)
            share_copy(k).start()

    def kernel_grad(k):
        turned[...] += lax.dot_general(
            act_all[k], taps[k], (((1,), (1,)), ((), ())), preferred_element_type=F32
        )

    def sum_x(dz):
        arrived(got_x.at[dz], r_share.at[dz])
        total = own_sum[dz]
        for j in range(3):
            total = total + got_x[dz, j].astype(F32)
        return total

    def pass_image(piece):
        arrived(images.at[FROM_PAIR, pieces_of_image[piece]], r_pair_img.at[piece])
        for j in (3, 2, 1):
            pass_copy(piece, j).start()

    across = copy(pair_out, pair_in, s_pair, r_pair, pair)

    def send_across(k):
        pair_out[...] = sum_x(1).astype(BF16)
        across.start()

    def finish(k):
        grad_ref[...] = turned[...].T * scale
        total = sum_x(0)
        across.wait_recv()
        total = total + pair_in[...].astype(F32)
        total = unpack(total, ROWS_A, keep.astype(F32)).T[:PIXELS].astype(BF16)
        out_ref[...] = total.reshape(out_ref.shape)

    stages = dict(
        A=next_conv,
        J=join,
        Y=sum_y,
        Z=sum_z,
        M=meet,
        P=spread_y,
        F=forward_y,
        C=second_conv,
        G=kernel_grad,
        R=pass_image,
        X=send_across,
        W=finish,
    )

    pl.semaphore_wait(barrier, len(peers))
    pair_copy(0).start()
    pair_copy(1).start()
    image_copy(3).start()
    sign = 1 - 2 * section
    pixel = lane // 2
    row = pixel // SIDE
    column = pixel - SIDE * row
    for tap in range(TAPS):
        there_row = row + sign * (tap // 3 - 1)
        there_column = column + sign * (tap % 3 - 1)
        inside = (there_row >= 0) & (there_row < SIDE) & (there_column >= 0) & (there_column < SIDE)
        inside = (inside & (lane < PIXELS)).astype(F32)
        masks_f[tap] = inside
        masks[tap] = inside.astype(BF16)
    load.wait()
    flipped[...] = k_ref[...].T
    first_conv(0)
    send_parts(0)
    image_copy(2).start()
    image_copy(1).start()
    turned[...] = jnp.zeros_like(turned)

    for stage, k in SCHEDULE:
        stages[stage](int(k))

    across.wait_send()
    left(images.at[pl.ds(0, 7)], s_img)
    round_sums = CHUNKS - len(STRAIGHT_SUMS)
    round_gathers = CHUNKS - len(STRAIGHT_GATHERS)
    for send in (s_relay, s_near, s_join):
        left(relayed.at[pl.ds(0, round_sums)], send)
    left(act.at[pl.ds(0, round_gathers), pl.ds(0, 2)], s_ay)
    left(act.at[pl.ds(0, round_gathers), 0], s_af)
    if STRAIGHT_SUMS:
        left(got_y.at[pl.ds(0, len(STRAIGHT_SUMS))], s_straight)
    if STRAIGHT_GATHERS:
        left(act.at[pl.ds(0, len(STRAIGHT_GATHERS)), pl.ds(0, 3)], s_gather)
    left(got_z, s_z)
    left(ex_out, s_ex)
    left(got_z, s_az)
    left(share.at[pl.ds(0, 6)], s_share)


def body(section_input, kernels):
    images, channels = section_input.shape[1], section_input.shape[4]
    inner = kernels.shape[4]
    scale = 1.0 / math.sqrt(CHUNKS * images * SIDE * SIDE)
    sem = pltpu.SemaphoreType.DMA
    pixels_first = section_input[0].transpose(1, 2, 0, 3).reshape(SIDE * SIDE, images, channels)
    out, grads = pl.pallas_call(
        functools.partial(kernel, scale),
        out_shape=(
            jax.ShapeDtypeStruct((SIDE * SIDE, images, channels), BF16),
            pltpu.VMEM((TAPS * channels, inner), F32),
        ),
        in_specs=[pl.BlockSpec(memory_space=pl.ANY)] * 2,
        out_specs=[pl.BlockSpec(memory_space=pltpu.VMEM)] * 2,
        scratch_shapes=[
            pltpu.VMEM((SIDE * SIDE, images, channels), BF16),
            pltpu.VMEM((TAPS * channels, inner), BF16),
            pltpu.VMEM((TAPS, 1, LANES), BF16),
            pltpu.VMEM((TAPS, 1, LANES), F32),
            pltpu.VMEM((CHUNKS, BLOCK_A, 128), BF16),
            pltpu.VMEM((CHUNKS, TAPS * channels, LANES), BF16),
            pltpu.VMEM((inner, TAPS * channels), BF16),
            pltpu.VMEM((CHUNKS, 4, 2, HALF, 128), BF16),
            pltpu.VMEM((CHUNKS, 4, 2, HALF, 128), F32),
            pltpu.VMEM((CHUNKS, 2, HALF, 128), BF16),
            pltpu.VMEM((CHUNKS, 2, HALF, 128), BF16),
            pltpu.VMEM((CHUNKS, 3, 2, HALF, 128), BF16),
            pltpu.VMEM((CHUNKS, 4, QUARTER, 128), BF16),
            pltpu.VMEM((CHUNKS, 4, QUARTER, 128), F32),
            pltpu.VMEM((CHUNKS, 3, QUARTER, 128), BF16),
            pltpu.VMEM((CHUNKS, QUARTER, 128), F32),
            pltpu.VMEM((CHUNKS, QUARTER, 128), BF16),
            pltpu.VMEM((CHUNKS, QUARTER, 128), BF16),
            pltpu.VMEM((CHUNKS, 4, 4, QUARTER, 128), BF16),
            pltpu.VMEM((CHUNKS, inner, LANES), BF16),
            pltpu.VMEM((CHUNKS, BLOCK_A, 128), BF16),
            pltpu.VMEM((2, 3, BLOCK_A, 128), BF16),
            pltpu.VMEM((2, BLOCK_A, 128), F32),
            pltpu.VMEM((BLOCK_A, 128), BF16),
            pltpu.VMEM((BLOCK_A, 128), BF16),
            pltpu.VMEM((inner, TAPS * channels), F32),
        ]
        + [sem] * 15
        + [sem((2,))]
        + [sem((CHUNKS,))] * 8
        + [sem((2,)), sem],
        compiler_params=pltpu.CompilerParams(
            collective_id=0, has_side_effects=True, vmem_limit_bytes=60 * 2**20
        ),
        name="relay",
    )(pixels_first, kernels.reshape(TAPS * channels, inner))
    out = out.reshape(SIDE, SIDE, images, channels).transpose(2, 0, 1, 3)
    return out[None], grads.reshape(kernels.shape)


def solution(mesh):
    return jax.shard_map(
        body,
        mesh=mesh,
        in_specs=(
            P("section", "narrow", None, None, "wide"),
            P("section", None, None, "wide", "narrow"),
        ),
        out_specs=(
            P("section", "narrow", None, None, "wide"),
            P("section", None, None, "wide", "narrow"),
        ),
        check_vma=False,
    )
```

```python
import functools
import math

import jax
import jax.numpy as jnp
from jax import lax
from jax.experimental import pallas as pl
from jax.experimental.pallas import tpu as pltpu
from jax.sharding import PartitionSpec as P

MESH = pl.DeviceIdType.MESH
BF16 = jnp.bfloat16
F32 = jnp.float32

SIDE = 14
CHUNKS = 8
PIXELS = 2 * SIDE * SIDE
LANES = 512
SPILL = PIXELS - 384
TAPS = 9
ROWS_A = 160
ROWS_B = 320
BLOCK_A = 3 * ROWS_A + 16
BLOCK_B = 3 * (ROWS_B // 4) + 16
HALF = BLOCK_B // 2
QUARTER = BLOCK_B // 4

SLOT = {(0, 0): 0, (0, 1): 1, (0, 2): 2, (1, 0): 3, (1, 1): 4, (1, 2): 5, (1, 3): 6, (0, 3): 7}
FROM_PAIR = SLOT[(1, 0)]

STRAIGHT_SUMS = (0, 1, 3, 4)
STRAIGHT_GATHERS = (4, 5, 6, 7)

SCHEDULE = (
    "A1", "R0", "R1", "A3", "Y0", "A4", "Y1", "A6", "Z0", "Y3", "A5", "M0", "A2", "Z1", "Y4", "M1", "J6",
    "A7", "J5", "Z3", "M3", "P0", "Z4", "J2", "Y6", "M4", "J7", "P1", "Y5", "P3", "Y2", "Z6", "M6", "P4",
    "Y7", "Z5", "Z2", "M5", "F3", "F1", "M2", "P6", "Z7", "C4", "P5", "M7", "C1", "G4", "C6", "P2", "P7",
    "C3", "C5", "F0", "G5", "F2", "G3", "G1", "G6", "X0", "C7", "C2", "G7", "C0", "G2", "G0", "W0",
)


def chunk_dz(k):
    return ((k + 1) // 4) % 2


def chunk_dx(k):
    late = k // 6
    return (1 - late) * (k % 3) + 3 * late


def silu(values):
    return values * jax.nn.sigmoid(values)


def silu_slope(values):
    logistic = jax.nn.sigmoid(values)
    return logistic * (1.0 + values * (1.0 - logistic))


def pack(values):
    rows = values.shape[0]
    spilled = values[:16, 384:]
    for group in range(1, rows // 16):
        spilled = spilled + pltpu.roll(values[16 * group : 16 * group + 16, 384:], SPILL * group, 1)
    return jnp.concatenate([values[:, 0:128], values[:, 128:256], values[:, 256:384], spilled], axis=0)


def unpack(block, rows, keep):
    spilled = block[3 * rows :]
    last = [spilled * keep]
    for group in range(1, rows // 16):
        last.append(pltpu.roll(spilled, 128 - SPILL * group, 1) * keep)
    parts = [block[0:rows], block[rows : 2 * rows], block[2 * rows : 3 * rows], jnp.concatenate(last, axis=0)]
    return jnp.concatenate(parts, axis=1)


def kernel(
    scale,
    x_hbm,
    k_hbm,
    out_ref,
    grad_ref,
    x_ref,
    k_ref,
    masks,
    masks_f,
    images,
    taps,
    flipped,
    part,
    part_f,
    relayed,
    joined,
    got_y,
    quarter,
    quarter_f,
    got_z,
    pre,
    ex_out,
    ex_in,
    act,
    act_all,
    share,
    got_x,
    own_sum,
    pair_out,
    pair_in,
    turned,
    s_load_x,
    s_load,
    s_img,
    s_relay,
    s_near,
    s_join,
    s_z,
    s_ex,
    s_az,
    s_ay,
    s_af,
    s_share,
    s_straight,
    s_gather,
    s_pair,
    r_pair_img,
    r_img,
    r_relay,
    r_y,
    r_z,
    r_ex,
    r_az,
    r_ay,
    r_af,
    r_share,
    r_pair,
):
    section = lax.axis_index("section")
    wide = lax.axis_index("wide")
    narrow = lax.axis_index("narrow")
    y, zl = wide // 4, wide % 4
    zh, x = narrow // 4, narrow % 4

    def at_y(j):
        return (section, ((y + j) % 4) * 4 + zl, narrow)

    def at_z(j):
        return (section, y * 4 + (zl + j) % 4, narrow)

    def at_x(j):
        return (section, wide, zh * 4 + (x + j) % 4)

    pair = (section, wide, (1 - zh) * 4 + x)
    other = (1 - section, wide, narrow)

    def copy(src, dst, send, recv, device):
        return pltpu.make_async_remote_copy(
            src_ref=src, dst_ref=dst, send_sem=send, recv_sem=recv, device_id=device, device_id_type=MESH
        )

    barrier = pltpu.get_barrier_semaphore()
    peers = [pair] + [at_z(j) for j in (2, 1, 3)] + [at_x(j) for j in (2, 1, 3)]
    peers += [at_y(j) for j in (2, 1, 3)] + [other]
    for peer in peers:
        pl.semaphore_signal(barrier, inc=1, device_id=peer, device_id_type=MESH)

    load_x = pltpu.make_async_copy(x_hbm, x_ref, s_load_x)
    load_x.start()
    load = pltpu.make_async_copy(k_hbm, k_ref, s_load)
    load.start()

    lane = lax.broadcasted_iota(jnp.int32, (1, LANES), 1)
    keep = (lane[:, :128] < SPILL).astype(BF16)

    def shift_of(tap, direction):
        offset = 2 * ((tap // 3 - 1) * SIDE + tap % 3 - 1)
        return (LANES - direction * offset) % LANES

    blank = jnp.zeros((LANES - PIXELS, ROWS_A), F32)
    load_x.wait()
    own_f = jnp.concatenate([x_ref[...].reshape(PIXELS, ROWS_A).astype(F32), blank], axis=0).T
    own = own_f.astype(BF16)
    images[0] = pack(own_f).astype(BF16)

    def image_copy(j):
        there = SLOT[(0, (4 - j) % 4)]
        return copy(images.at[0], images.at[there], s_img, r_img.at[there], at_x(j))

    pieces_of_image = (pl.ds(0, 256), pl.ds(256, BLOCK_A - 256))

    def pair_copy(piece):
        rows = pieces_of_image[piece]
        there = images.at[FROM_PAIR, rows]
        return copy(images.at[0, rows], there, s_img, r_pair_img.at[piece], pair)

    def pass_copy(piece, j):
        rows = pieces_of_image[piece]
        slot = SLOT[(1, (4 - j) % 4)]
        return copy(images.at[FROM_PAIR, rows], images.at[slot, rows], s_img, r_img.at[slot], at_x(j))

    def relay_copy(k, half):
        return copy(
            part.at[k, (y + 2) % 4, half], relayed.at[k, half], s_relay, r_relay.at[k], at_y(1 + 2 * half)
        )

    def near_copy(k, half):
        j = 3 - 2 * half
        return copy(part.at[k, (y + j) % 4, half], got_y.at[k, 0, half], s_near, r_y.at[k], at_y(j))

    def straight_copy(k, j):
        return copy(part.at[k, (y + j) % 4], got_y.at[k, j - 1], s_straight, r_y.at[k], at_y(j))

    def gather_copy(k, j):
        here = act.at[k, y]
        return copy(here, here, s_gather, r_ay.at[k], at_y(j))

    def join_copy(k, half):
        return copy(joined.at[k, half], got_y.at[k, 1, half], s_join, r_y.at[k], at_y(1 + 2 * half))

    def z_copy(k, j):
        return copy(quarter.at[k, (zl + j) % 4], got_z.at[k, j - 1], s_z, r_z.at[k], at_z(j))

    def ex_copy(k):
        return copy(ex_out.at[k], ex_in.at[k], s_ex, r_ex.at[k], other)

    def az_copy(k, j):
        here = act.at[k, y, zl]
        return copy(here, here, s_az, r_az.at[k], at_z(j))

    def ay_copy(k, side):
        here = act.at[k, y]
        return copy(here, here, s_ay, r_ay.at[k], at_y(1 + 2 * side))

    def af_copy(k, side):
        here = act.at[k, (y + 3 - 2 * side) % 4, pl.ds(2 * side, 2)]
        return copy(here, here, s_af, r_af.at[k], at_y(1 + 2 * side))

    def share_copy(k):
        dz, dx = chunk_dz(k), chunk_dx(k)
        return copy(share.at[k], got_x.at[dz, 3 - dx], s_share, r_share.at[dz], at_x(dx))

    def arrived(buffer, recv):
        copy(buffer, buffer, s_pair, recv, other).wait_recv()

    def left(buffer, send):
        copy(buffer, buffer, send, r_pair, other).wait_send()

    def first_conv(k):
        image = own if k == 0 else unpack(images[k], ROWS_A, keep)
        for tap in range(TAPS):
            moved = image
            if tap != 4:
                moved = pltpu.roll(image, shift_of(tap, sign), 1) * masks[tap]
            taps[k, pl.ds(ROWS_A * tap, ROWS_A), :] = moved
        total = jnp.dot(flipped[...], taps[k], preferred_element_type=F32)
        for block in range(4):
            piece = pack(total[80 * block : 80 * block + 80])
            for half in range(2):
                rows = piece[HALF * half : HALF * half + HALF]
                part_f[k, block, half] = rows
                part[k, block, half] = rows.astype(BF16)

    def send_parts(k):
        if k in STRAIGHT_SUMS:
            for j in (2, 1, 3):
                straight_copy(k, j).start()
            return
        for half in range(2):
            relay_copy(k, half).start()
        for half in range(2):
            near_copy(k, half).start()

    def next_conv(k):
        if k != FROM_PAIR:
            arrived(images.at[k], r_img.at[k])

        first_conv(k)
        send_parts(k)

    def join(k):
        arrived(relayed.at[k], r_relay.at[k])
        for half in range(2):
            total = part_f[k, (y + 1 + 2 * half) % 4, half] + relayed[k, half].astype(F32)
            joined[k, half] = total.astype(BF16)
            join_copy(k, half).start()

    def sum_y(k):
        pieces = 3 if k in STRAIGHT_SUMS else 2
        arrived(got_y.at[k, pl.ds(0, pieces)], r_y.at[k])
        for half in range(2):
            total = part_f[k, y, half]
            for j in range(pieces):
                total = total + got_y[k, j, half].astype(F32)
            for side in range(2):
                piece = total[QUARTER * side : QUARTER * side + QUARTER]
                quarter_f[k, 2 * half + side] = piece
                quarter[k, 2 * half + side] = piece.astype(BF16)
        for j in (2, 3, 1):
            z_copy(k, j).start()

    def sum_z(k):
        arrived(got_z.at[k], r_z.at[k])
        total = quarter_f[k, zl]
        for j in range(3):
            total = total + got_z[k, j].astype(F32)
        pre[k] = total
        ex_out[k] = jnp.where(section == 0, silu(total), total).astype(BF16)
        ex_copy(k).start()

    def meet(k):
        arrived(ex_in.at[k], r_ex.at[k])
        incoming = ex_in[k].astype(F32)
        received = jnp.where(section == 0, incoming * silu_slope(pre[k]), incoming)
        act[k, y, zl] = received.astype(BF16)
        for j in (2, 3, 1):
            az_copy(k, j).start()

    def spread_y(k):
        arrived(got_z.at[k], r_az.at[k])
        if k in STRAIGHT_GATHERS:
            for j in (2, 1, 3):
                gather_copy(k, j).start()
            return
        for side in range(2):
            ay_copy(k, side).start()

    def forward_y(k):
        arrived(act.at[k, pl.ds(0, 2)], r_ay.at[k])
        for side in range(2):
            af_copy(k, side).start()

    def second_conv(k):
        if k in STRAIGHT_GATHERS:
            arrived(act.at[k, pl.ds(0, 3)], r_ay.at[k])
        else:
            arrived(act.at[k, 0], r_af.at[k])
        for block in range(4):
            piece = unpack(act[k, block].reshape(BLOCK_B, 128), 80, keep)
            act_all[k, pl.ds(80 * block, 80), :] = piece
        total = None
        for line in (1, 0, 2):
            rows = pl.ds(3 * ROWS_A * line, 3 * ROWS_A)
            product = jnp.dot(k_ref[rows], act_all[k], preferred_element_type=F32)
            for place in range(3):
                tap = 3 * line + place
                moved = product[ROWS_A * place : ROWS_A * place + ROWS_A]
                if tap != 4:
                    moved = pltpu.roll(moved, shift_of(tap, -sign), 1) * masks_f[8 - tap]
                total = moved if total is None else total + moved
        block = pack(total)
        dz, dx = chunk_dz(k), chunk_dx(k)
        if dx == 0:
            own_sum[dz] = block
        else:
            share[k] = block.astype(BF16)
            share_copy(k).start()

    def kernel_grad(k):
        turned[...] += lax.dot_general(
            act_all[k], taps[k], (((1,), (1,)), ((), ())), preferred_element_type=F32
        )

    def sum_x(dz):
        arrived(got_x.at[dz], r_share.at[dz])
        total = own_sum[dz]
        for j in range(3):
            total = total + got_x[dz, j].astype(F32)
        return total

    def pass_image(piece):
        arrived(images.at[FROM_PAIR, pieces_of_image[piece]], r_pair_img.at[piece])
        for j in (3, 2, 1):
            pass_copy(piece, j).start()

    across = copy(pair_out, pair_in, s_pair, r_pair, pair)

    def send_across(k):
        pair_out[...] = sum_x(1).astype(BF16)
        across.start()

    def finish(k):
        grad_ref[...] = turned[...].T * scale
        total = sum_x(0)
        across.wait_recv()
        total = total + pair_in[...].astype(F32)
        total = unpack(total, ROWS_A, keep.astype(F32)).T[:PIXELS].astype(BF16)
        out_ref[...] = total.reshape(out_ref.shape)

    stages = dict(
        A=next_conv,
        J=join,
        Y=sum_y,
        Z=sum_z,
        M=meet,
        P=spread_y,
        F=forward_y,
        C=second_conv,
        G=kernel_grad,
        R=pass_image,
        X=send_across,
        W=finish,
    )

    pl.semaphore_wait(barrier, len(peers))
    pair_copy(0).start()
    pair_copy(1).start()
    image_copy(3).start()
    sign = 1 - 2 * section
    pixel = lane // 2
    row = pixel // SIDE
    column = pixel - SIDE * row
    for tap in range(TAPS):
        there_row = row + sign * (tap // 3 - 1)
        there_column = column + sign * (tap % 3 - 1)
        inside = (there_row >= 0) & (there_row < SIDE) & (there_column >= 0) & (there_column < SIDE)
        inside = (inside & (lane < PIXELS)).astype(F32)
        masks_f[tap] = inside
        masks[tap] = inside.astype(BF16)
    load.wait()
    flipped[...] = k_ref[...].T
    first_conv(0)
    send_parts(0)
    image_copy(2).start()
    image_copy(1).start()
    turned[...] = jnp.zeros_like(turned)

    for stage, k in SCHEDULE:
        stages[stage](int(k))

    across.wait_send()
    left(images.at[pl.ds(0, 7)], s_img)
    round_sums = CHUNKS - len(STRAIGHT_SUMS)
    round_gathers = CHUNKS - len(STRAIGHT_GATHERS)
    for send in (s_relay, s_near, s_join):
        left(relayed.at[pl.ds(0, round_sums)], send)
    left(act.at[pl.ds(0, round_gathers), pl.ds(0, 2)], s_ay)
    left(act.at[pl.ds(0, round_gathers), 0], s_af)
    if STRAIGHT_SUMS:
        left(got_y.at[pl.ds(0, len(STRAIGHT_SUMS))], s_straight)
    if STRAIGHT_GATHERS:
        left(act.at[pl.ds(0, len(STRAIGHT_GATHERS)), pl.ds(0, 3)], s_gather)
    left(got_z, s_z)
    left(ex_out, s_ex)
    left(got_z, s_az)
    left(share.at[pl.ds(0, 6)], s_share)


def body(section_input, kernels):
    images, channels = section_input.shape[1], section_input.shape[4]
    inner = kernels.shape[4]
    scale = 1.0 / math.sqrt(CHUNKS * images * SIDE * SIDE)
    sem = pltpu.SemaphoreType.DMA
    pixels_first = section_input[0].transpose(1, 2, 0, 3).reshape(SIDE * SIDE, images, channels)
    out, grads = pl.pallas_call(
        functools.partial(kernel, scale),
        out_shape=(
            pltpu.VMEM((SIDE * SIDE, images, channels), BF16),
            pltpu.VMEM((TAPS * channels, inner), F32),
        ),
        in_specs=[pl.BlockSpec(memory_space=pl.ANY)] * 2,
        out_specs=[pl.BlockSpec(memory_space=pltpu.VMEM)] * 2,
        scratch_shapes=[
            pltpu.VMEM((SIDE * SIDE, images, channels), BF16),
            pltpu.VMEM((TAPS * channels, inner), BF16),
            pltpu.VMEM((TAPS, 1, LANES), BF16),
            pltpu.VMEM((TAPS, 1, LANES), F32),
            pltpu.VMEM((CHUNKS, BLOCK_A, 128), BF16),
            pltpu.VMEM((CHUNKS, TAPS * channels, LANES), BF16),
            pltpu.VMEM((inner, TAPS * channels), BF16),
            pltpu.VMEM((CHUNKS, 4, 2, HALF, 128), BF16),
            pltpu.VMEM((CHUNKS, 4, 2, HALF, 128), F32),
            pltpu.VMEM((CHUNKS, 2, HALF, 128), BF16),
            pltpu.VMEM((CHUNKS, 2, HALF, 128), BF16),
            pltpu.VMEM((CHUNKS, 3, 2, HALF, 128), BF16),
            pltpu.VMEM((CHUNKS, 4, QUARTER, 128), BF16),
            pltpu.VMEM((CHUNKS, 4, QUARTER, 128), F32),
            pltpu.VMEM((CHUNKS, 3, QUARTER, 128), BF16),
            pltpu.VMEM((CHUNKS, QUARTER, 128), F32),
            pltpu.VMEM((CHUNKS, QUARTER, 128), BF16),
            pltpu.VMEM((CHUNKS, QUARTER, 128), BF16),
            pltpu.VMEM((CHUNKS, 4, 4, QUARTER, 128), BF16),
            pltpu.VMEM((CHUNKS, inner, LANES), BF16),
            pltpu.VMEM((CHUNKS, BLOCK_A, 128), BF16),
            pltpu.VMEM((2, 3, BLOCK_A, 128), BF16),
            pltpu.VMEM((2, BLOCK_A, 128), F32),
            pltpu.VMEM((BLOCK_A, 128), BF16),
            pltpu.VMEM((BLOCK_A, 128), BF16),
            pltpu.VMEM((inner, TAPS * channels), F32),
        ]
        + [sem] * 15
        + [sem((2,))]
        + [sem((CHUNKS,))] * 8
        + [sem((2,)), sem],
        compiler_params=pltpu.CompilerParams(
            collective_id=0, has_side_effects=True, vmem_limit_bytes=60 * 2**20
        ),
        name="relay",
    )(pixels_first, kernels.reshape(TAPS * channels, inner))
    out = out.reshape(SIDE, SIDE, images, channels).transpose(2, 0, 1, 3)
    return out[None], grads.reshape(kernels.shape)


def solution(mesh):
    return jax.shard_map(
        body,
        mesh=mesh,
        in_specs=(
            P("section", "narrow", None, None, "wide"),
            P("section", None, None, "wide", "narrow"),
        ),
        out_specs=(
            P("section", "narrow", None, None, "wide"),
            P("section", None, None, "wide", "narrow"),
        ),
        check_vma=False,
    )
```

```python
import functools
import math

import jax
import jax.numpy as jnp
from jax import lax
from jax.experimental import pallas as pl
from jax.experimental.pallas import tpu as pltpu
from jax.sharding import PartitionSpec as P

MESH = pl.DeviceIdType.MESH
BF16 = jnp.bfloat16
F32 = jnp.float32

SIDE = 14
CHUNKS = 8
PIXELS = 2 * SIDE * SIDE
LANES = 512
SPILL = PIXELS - 384
TAPS = 9
ROWS_A = 160
ROWS_B = 320
BLOCK_A = 3 * ROWS_A + 16
BLOCK_B = 3 * (ROWS_B // 4) + 16
HALF = BLOCK_B // 2
QUARTER = BLOCK_B // 4

SLOT = {(0, 0): 0, (0, 1): 1, (0, 2): 2, (1, 0): 3, (1, 1): 4, (1, 2): 5, (1, 3): 6, (0, 3): 7}
FROM_PAIR = SLOT[(1, 0)]

STRAIGHT_SUMS = (0, 1, 3, 4)
STRAIGHT_GATHERS = (4, 5, 6, 7)

SCHEDULE = (
    "A1", "R0", "R1", "A3", "Y0", "A4", "Y1", "A6", "Z0", "Y3", "A5", "M0", "A2", "Z1", "Y4", "M1", "J6",
    "A7", "J5", "Z3", "M3", "P0", "Z4", "J2", "Y6", "M4", "J7", "P1", "Y5", "P3", "Y2", "Z6", "M6", "P4",
    "Y7", "Z5", "Z2", "M5", "F3", "F1", "M2", "P6", "Z7", "P5", "M7", "C4", "C1", "C6", "P2", "P7", "G4",
    "C5", "F0", "C3", "F2", "G5", "G3", "G1", "G6", "X0", "C7", "C2", "G7", "C0", "G2", "G0", "W0",
)


def chunk_dz(k):
    return ((k + 1) // 4) % 2


def chunk_dx(k):
    late = k // 6
    return (1 - late) * (k % 3) + 3 * late


def silu(values):
    return values * jax.nn.sigmoid(values)


def silu_slope(values):
    logistic = jax.nn.sigmoid(values)
    return logistic * (1.0 + values * (1.0 - logistic))


def pack(values):
    rows = values.shape[0]
    spilled = values[:16, 384:]
    for group in range(1, rows // 16):
        spilled = spilled + pltpu.roll(values[16 * group : 16 * group + 16, 384:], SPILL * group, 1)
    return jnp.concatenate([values[:, 0:128], values[:, 128:256], values[:, 256:384], spilled], axis=0)


def unpack(block, rows, keep):
    spilled = block[3 * rows :]
    last = [spilled * keep]
    for group in range(1, rows // 16):
        last.append(pltpu.roll(spilled, 128 - SPILL * group, 1) * keep)
    parts = [block[0:rows], block[rows : 2 * rows], block[2 * rows : 3 * rows], jnp.concatenate(last, axis=0)]
    return jnp.concatenate(parts, axis=1)


def kernel(
    scale,
    x_hbm,
    k_hbm,
    out_ref,
    grad_ref,
    x_ref,
    k_ref,
    masks,
    masks_f,
    images,
    taps,
    flipped,
    part,
    part_f,
    relayed,
    joined,
    got_y,
    quarter,
    quarter_f,
    got_z,
    pre,
    ex_out,
    ex_in,
    act,
    act_all,
    share,
    got_x,
    own_sum,
    pair_out,
    pair_in,
    turned,
    s_load_x,
    s_load,
    s_img,
    s_relay,
    s_near,
    s_join,
    s_z,
    s_ex,
    s_az,
    s_ay,
    s_af,
    s_share,
    s_straight,
    s_gather,
    s_pair,
    r_pair_img,
    r_img,
    r_relay,
    r_y,
    r_z,
    r_ex,
    r_az,
    r_ay,
    r_af,
    r_share,
    r_pair,
):
    section = lax.axis_index("section")
    wide = lax.axis_index("wide")
    narrow = lax.axis_index("narrow")
    y, zl = wide // 4, wide % 4
    zh, x = narrow // 4, narrow % 4

    def at_y(j):
        return (section, ((y + j) % 4) * 4 + zl, narrow)

    def at_z(j):
        return (section, y * 4 + (zl + j) % 4, narrow)

    def at_x(j):
        return (section, wide, zh * 4 + (x + j) % 4)

    pair = (section, wide, (1 - zh) * 4 + x)
    other = (1 - section, wide, narrow)

    def copy(src, dst, send, recv, device):
        return pltpu.make_async_remote_copy(
            src_ref=src, dst_ref=dst, send_sem=send, recv_sem=recv, device_id=device, device_id_type=MESH
        )

    barrier = pltpu.get_barrier_semaphore()
    peers = [pair] + [at_z(j) for j in (2, 1, 3)] + [at_x(j) for j in (2, 1, 3)]
    peers += [at_y(j) for j in (2, 1, 3)] + [other]
    for peer in peers:
        pl.semaphore_signal(barrier, inc=1, device_id=peer, device_id_type=MESH)

    load_x = pltpu.make_async_copy(x_hbm, x_ref, s_load_x)
    load_x.start()
    load = pltpu.make_async_copy(k_hbm, k_ref, s_load)
    load.start()

    lane = lax.broadcasted_iota(jnp.int32, (1, LANES), 1)
    keep = (lane[:, :128] < SPILL).astype(BF16)

    def shift_of(tap, direction):
        offset = 2 * ((tap // 3 - 1) * SIDE + tap % 3 - 1)
        return (LANES - direction * offset) % LANES

    blank = jnp.zeros((LANES - PIXELS, ROWS_A), F32)
    load_x.wait()
    own_f = jnp.concatenate([x_ref[...].reshape(PIXELS, ROWS_A).astype(F32), blank], axis=0).T
    own = own_f.astype(BF16)
    images[0] = pack(own_f).astype(BF16)

    def image_copy(j):
        there = SLOT[(0, (4 - j) % 4)]
        return copy(images.at[0], images.at[there], s_img, r_img.at[there], at_x(j))

    pieces_of_image = (pl.ds(0, 256), pl.ds(256, BLOCK_A - 256))

    def pair_copy(piece):
        rows = pieces_of_image[piece]
        there = images.at[FROM_PAIR, rows]
        return copy(images.at[0, rows], there, s_img, r_pair_img.at[piece], pair)

    def pass_copy(piece, j):
        rows = pieces_of_image[piece]
        slot = SLOT[(1, (4 - j) % 4)]
        return copy(images.at[FROM_PAIR, rows], images.at[slot, rows], s_img, r_img.at[slot], at_x(j))

    def relay_copy(k, half):
        return copy(
            part.at[k, (y + 2) % 4, half], relayed.at[k, half], s_relay, r_relay.at[k], at_y(1 + 2 * half)
        )

    def near_copy(k, half):
        j = 3 - 2 * half
        return copy(part.at[k, (y + j) % 4, half], got_y.at[k, 0, half], s_near, r_y.at[k], at_y(j))

    def straight_copy(k, j):
        return copy(part.at[k, (y + j) % 4], got_y.at[k, j - 1], s_straight, r_y.at[k], at_y(j))

    def gather_copy(k, j):
        here = act.at[k, y]
        return copy(here, here, s_gather, r_ay.at[k], at_y(j))

    def join_copy(k, half):
        return copy(joined.at[k, half], got_y.at[k, 1, half], s_join, r_y.at[k], at_y(1 + 2 * half))

    def z_copy(k, j):
        return copy(quarter.at[k, (zl + j) % 4], got_z.at[k, j - 1], s_z, r_z.at[k], at_z(j))

    def ex_copy(k):
        return copy(ex_out.at[k], ex_in.at[k], s_ex, r_ex.at[k], other)

    def az_copy(k, j):
        here = act.at[k, y, zl]
        return copy(here, here, s_az, r_az.at[k], at_z(j))

    def ay_copy(k, side):
        here = act.at[k, y]
        return copy(here, here, s_ay, r_ay.at[k], at_y(1 + 2 * side))

    def af_copy(k, side):
        here = act.at[k, (y + 3 - 2 * side) % 4, pl.ds(2 * side, 2)]
        return copy(here, here, s_af, r_af.at[k], at_y(1 + 2 * side))

    def share_copy(k):
        dz, dx = chunk_dz(k), chunk_dx(k)
        return copy(share.at[k], got_x.at[dz, 3 - dx], s_share, r_share.at[dz], at_x(dx))

    def arrived(buffer, recv):
        copy(buffer, buffer, s_pair, recv, other).wait_recv()

    def left(buffer, send):
        copy(buffer, buffer, send, r_pair, other).wait_send()

    def first_conv(k):
        image = own if k == 0 else unpack(images[k], ROWS_A, keep)
        for tap in range(TAPS):
            moved = image
            if tap != 4:
                moved = pltpu.roll(image, shift_of(tap, sign), 1) * masks[tap]
            taps[k, pl.ds(ROWS_A * tap, ROWS_A), :] = moved
        total = jnp.dot(flipped[...], taps[k], preferred_element_type=F32)
        for block in range(4):
            piece = pack(total[80 * block : 80 * block + 80])
            for half in range(2):
                rows = piece[HALF * half : HALF * half + HALF]
                part_f[k, block, half] = rows
                part[k, block, half] = rows.astype(BF16)

    def send_parts(k):
        if k in STRAIGHT_SUMS:
            for j in (2, 1, 3):
                straight_copy(k, j).start()
            return
        for half in range(2):
            relay_copy(k, half).start()
        for half in range(2):
            near_copy(k, half).start()

    def next_conv(k):
        if k != FROM_PAIR:
            arrived(images.at[k], r_img.at[k])

        first_conv(k)
        send_parts(k)

    def join(k):
        arrived(relayed.at[k], r_relay.at[k])
        for half in range(2):
            total = part_f[k, (y + 1 + 2 * half) % 4, half] + relayed[k, half].astype(F32)
            joined[k, half] = total.astype(BF16)
            join_copy(k, half).start()

    def sum_y(k):
        pieces = 3 if k in STRAIGHT_SUMS else 2
        arrived(got_y.at[k, pl.ds(0, pieces)], r_y.at[k])
        for half in range(2):
            total = part_f[k, y, half]
            for j in range(pieces):
                total = total + got_y[k, j, half].astype(F32)
            for side in range(2):
                piece = total[QUARTER * side : QUARTER * side + QUARTER]
                quarter_f[k, 2 * half + side] = piece
                quarter[k, 2 * half + side] = piece.astype(BF16)
        for j in (2, 3, 1):
            z_copy(k, j).start()

    def sum_z(k):
        arrived(got_z.at[k], r_z.at[k])
        total = quarter_f[k, zl]
        for j in range(3):
            total = total + got_z[k, j].astype(F32)
        pre[k] = total
        ex_out[k] = jnp.where(section == 0, silu(total), total).astype(BF16)
        ex_copy(k).start()

    def meet(k):
        arrived(ex_in.at[k], r_ex.at[k])
        incoming = ex_in[k].astype(F32)
        received = jnp.where(section == 0, incoming * silu_slope(pre[k]), incoming)
        act[k, y, zl] = received.astype(BF16)
        for j in (2, 3, 1):
            az_copy(k, j).start()

    def spread_y(k):
        arrived(got_z.at[k], r_az.at[k])
        if k in STRAIGHT_GATHERS:
            for j in (2, 1, 3):
                gather_copy(k, j).start()
            return
        for side in range(2):
            ay_copy(k, side).start()

    def forward_y(k):
        arrived(act.at[k, pl.ds(0, 2)], r_ay.at[k])
        for side in range(2):
            af_copy(k, side).start()

    def second_conv(k):
        if k in STRAIGHT_GATHERS:
            arrived(act.at[k, pl.ds(0, 3)], r_ay.at[k])
        else:
            arrived(act.at[k, 0], r_af.at[k])
        for block in range(4):
            piece = unpack(act[k, block].reshape(BLOCK_B, 128), 80, keep)
            act_all[k, pl.ds(80 * block, 80), :] = piece
        total = None
        for line in (1, 0, 2):
            rows = pl.ds(3 * ROWS_A * line, 3 * ROWS_A)
            product = jnp.dot(k_ref[rows], act_all[k], preferred_element_type=F32)
            for place in range(3):
                tap = 3 * line + place
                moved = product[ROWS_A * place : ROWS_A * place + ROWS_A]
                if tap != 4:
                    moved = pltpu.roll(moved, shift_of(tap, -sign), 1) * masks_f[8 - tap]
                total = moved if total is None else total + moved
        block = pack(total)
        dz, dx = chunk_dz(k), chunk_dx(k)
        if dx == 0:
            own_sum[dz] = block
        else:
            share[k] = block.astype(BF16)
            share_copy(k).start()

    def kernel_grad(k):
        turned[...] += lax.dot_general(
            act_all[k], taps[k], (((1,), (1,)), ((), ())), preferred_element_type=F32
        )

    def sum_x(dz):
        arrived(got_x.at[dz], r_share.at[dz])
        total = own_sum[dz]
        for j in range(3):
            total = total + got_x[dz, j].astype(F32)
        return total

    def pass_image(piece):
        arrived(images.at[FROM_PAIR, pieces_of_image[piece]], r_pair_img.at[piece])
        for j in (3, 2, 1):
            pass_copy(piece, j).start()

    across = copy(pair_out, pair_in, s_pair, r_pair, pair)

    def send_across(k):
        pair_out[...] = sum_x(1).astype(BF16)
        across.start()

    def finish(k):
        grad_ref[...] = turned[...].T * scale
        total = sum_x(0)
        across.wait_recv()
        total = total + pair_in[...].astype(F32)
        total = unpack(total, ROWS_A, keep.astype(F32)).T[:PIXELS].astype(BF16)
        out_ref[...] = total.reshape(out_ref.shape)

    stages = dict(
        A=next_conv,
        J=join,
        Y=sum_y,
        Z=sum_z,
        M=meet,
        P=spread_y,
        F=forward_y,
        C=second_conv,
        G=kernel_grad,
        R=pass_image,
        X=send_across,
        W=finish,
    )

    pl.semaphore_wait(barrier, len(peers))
    pair_copy(0).start()
    pair_copy(1).start()
    image_copy(3).start()
    sign = 1 - 2 * section
    pixel = lane // 2
    row = pixel // SIDE
    column = pixel - SIDE * row
    for tap in range(TAPS):
        there_row = row + sign * (tap // 3 - 1)
        there_column = column + sign * (tap % 3 - 1)
        inside = (there_row >= 0) & (there_row < SIDE) & (there_column >= 0) & (there_column < SIDE)
        inside = (inside & (lane < PIXELS)).astype(F32)
        masks_f[tap] = inside
        masks[tap] = inside.astype(BF16)
    load.wait()
    flipped[...] = k_ref[...].T
    first_conv(0)
    send_parts(0)
    image_copy(2).start()
    image_copy(1).start()
    turned[...] = jnp.zeros_like(turned)

    for stage, k in SCHEDULE:
        stages[stage](int(k))

    across.wait_send()
    left(images.at[pl.ds(0, 7)], s_img)
    round_sums = CHUNKS - len(STRAIGHT_SUMS)
    round_gathers = CHUNKS - len(STRAIGHT_GATHERS)
    for send in (s_relay, s_near, s_join):
        left(relayed.at[pl.ds(0, round_sums)], send)
    left(act.at[pl.ds(0, round_gathers), pl.ds(0, 2)], s_ay)
    left(act.at[pl.ds(0, round_gathers), 0], s_af)
    if STRAIGHT_SUMS:
        left(got_y.at[pl.ds(0, len(STRAIGHT_SUMS))], s_straight)
    if STRAIGHT_GATHERS:
        left(act.at[pl.ds(0, len(STRAIGHT_GATHERS)), pl.ds(0, 3)], s_gather)
    left(got_z, s_z)
    left(ex_out, s_ex)
    left(got_z, s_az)
    left(share.at[pl.ds(0, 6)], s_share)


def body(section_input, kernels):
    images, channels = section_input.shape[1], section_input.shape[4]
    inner = kernels.shape[4]
    scale = 1.0 / math.sqrt(CHUNKS * images * SIDE * SIDE)
    sem = pltpu.SemaphoreType.DMA
    pixels_first = section_input[0].transpose(1, 2, 0, 3).reshape(SIDE * SIDE, images, channels)
    out, grads = pl.pallas_call(
        functools.partial(kernel, scale),
        out_shape=(
            pltpu.VMEM((SIDE * SIDE, images, channels), BF16),
            pltpu.VMEM((TAPS * channels, inner), F32),
        ),
        in_specs=[pl.BlockSpec(memory_space=pl.ANY)] * 2,
        out_specs=[pl.BlockSpec(memory_space=pltpu.VMEM)] * 2,
        scratch_shapes=[
            pltpu.VMEM((SIDE * SIDE, images, channels), BF16),
            pltpu.VMEM((TAPS * channels, inner), BF16),
            pltpu.VMEM((TAPS, 1, LANES), BF16),
            pltpu.VMEM((TAPS, 1, LANES), F32),
            pltpu.VMEM((CHUNKS, BLOCK_A, 128), BF16),
            pltpu.VMEM((CHUNKS, TAPS * channels, LANES), BF16),
            pltpu.VMEM((inner, TAPS * channels), BF16),
            pltpu.VMEM((CHUNKS, 4, 2, HALF, 128), BF16),
            pltpu.VMEM((CHUNKS, 4, 2, HALF, 128), F32),
            pltpu.VMEM((CHUNKS, 2, HALF, 128), BF16),
            pltpu.VMEM((CHUNKS, 2, HALF, 128), BF16),
            pltpu.VMEM((CHUNKS, 3, 2, HALF, 128), BF16),
            pltpu.VMEM((CHUNKS, 4, QUARTER, 128), BF16),
            pltpu.VMEM((CHUNKS, 4, QUARTER, 128), F32),
            pltpu.VMEM((CHUNKS, 3, QUARTER, 128), BF16),
            pltpu.VMEM((CHUNKS, QUARTER, 128), F32),
            pltpu.VMEM((CHUNKS, QUARTER, 128), BF16),
            pltpu.VMEM((CHUNKS, QUARTER, 128), BF16),
            pltpu.VMEM((CHUNKS, 4, 4, QUARTER, 128), BF16),
            pltpu.VMEM((CHUNKS, inner, LANES), BF16),
            pltpu.VMEM((CHUNKS, BLOCK_A, 128), BF16),
            pltpu.VMEM((2, 3, BLOCK_A, 128), BF16),
            pltpu.VMEM((2, BLOCK_A, 128), F32),
            pltpu.VMEM((BLOCK_A, 128), BF16),
            pltpu.VMEM((BLOCK_A, 128), BF16),
            pltpu.VMEM((inner, TAPS * channels), F32),
        ]
        + [sem] * 15
        + [sem((2,))]
        + [sem((CHUNKS,))] * 8
        + [sem((2,)), sem],
        compiler_params=pltpu.CompilerParams(
            collective_id=0, has_side_effects=True, vmem_limit_bytes=60 * 2**20
        ),
        name="relay",
    )(pixels_first, kernels.reshape(TAPS * channels, inner))
    out = out.reshape(SIDE, SIDE, images, channels).transpose(2, 0, 1, 3)
    return out[None], grads.reshape(kernels.shape)


def solution(mesh):
    return jax.shard_map(
        body,
        mesh=mesh,
        in_specs=(
            P("section", "narrow", None, None, "wide"),
            P("section", None, None, "wide", "narrow"),
        ),
        out_specs=(
            P("section", "narrow", None, None, "wide"),
            P("section", None, None, "wide", "narrow"),
        ),
        check_vma=False,
    )
```
